512 devices in a mesh: snode: 64 (over x, z), rowblk: 8 (over y, core).
Axes of the slice: x: 4, y: 4, z: 16, core: 2. Of those that a mesh axis runs over, the one named last changes fastest.
Arguments:
- rhs: float32 [4, 64, 256, 64], P(None, 'snode', 'rowblk'), may hold values from -6 to 6
- diag_inverse: float32 [4, 64, 256, 256], P(None, 'snode', 'rowblk')
- panels: bfloat16 [3, 64, 32, 256, 256], P(None, 'snode', None, 'rowblk'), may hold values from -0.125 to 0.125
- targets: int32 [3, 64, 32], P(None, 'snode'), may hold values from 64 to 254, as said below
- counts: int32 [3, 64], P(None, 'snode'), may hold values from 1 to 32
Outputs:
- solution: float32 [4, 64, 256, 64], P(None, 'snode', 'rowblk')
The draws below stay inside these ranges and needn't reach their ends.
Inputs may be any that keep to these rules, and one draw needn't show every extreme that they name: `targets`: a block of supernode n at level h names an ancestor of n in the elimination tree: for some k from 1 to 3 - h it is (h + k) * 64 + ((n with its lowest k bits cleared) XOR (k odd ? 64 / 2 : 0)).
All inputs are finite; a program needn't handle non-finite values.
Results may differ from the reference program's by a relative error of at most 0.0034.
Values may be sent and summed in bfloat16 or wider, within the bound.
A program may use at most 64 MiB of HBM per device.

```python
import math
import jax
import jax.numpy as jnp
from jax import lax

W = 256
R = 64
LV = 4
PB = 32
NODES = 64


def draw_diag_inverse(key, part):
    key = jax.random.fold_in(key, 5)
    first_key, second_key = jax.random.split(key)
    dims = (LV, NODES, W, W)
    spread = jax.random.normal(first_key, dims, jnp.float32)
    row_ids = lax.broadcasted_iota(jnp.int32, dims, 2)
    col_ids = lax.broadcasted_iota(jnp.int32, dims, 3)
    below_mask = (col_ids < row_ids).astype(jnp.float32)
    on_diagonal = (col_ids == row_ids).astype(jnp.float32)
    diagonal = jax.random.uniform(second_key, dims, jnp.float32, 0.6, 1.4)
    return spread * below_mask * (0.6 / math.sqrt(W)) + diagonal * on_diagonal


def draw_targets(key, part):
    key = jax.random.fold_in(key, 11)
    dims = (LV - 1, NODES, PB)
    height = lax.broadcasted_iota(jnp.int32, dims, 0)
    node_ids = lax.broadcasted_iota(jnp.int32, dims, 1)
    block_ids = lax.broadcasted_iota(jnp.int32, dims, 2)
    reach = LV - 1 - height
    picked = jax.random.randint(key, dims, 0, 1 << 20) % reach + 1
    distance = jnp.where(block_ids == 0, reach, jnp.where(block_ids == 1, 1, picked)).astype(jnp.int32)
    cleared = jnp.left_shift(jnp.right_shift(node_ids, distance), distance)
    flipped = distance % 2 * (NODES // 2)
    ancestor = jnp.bitwise_xor(cleared, flipped.astype(jnp.int32))
    return ((height + distance) * NODES + ancestor).astype(jnp.int32)


def with_ends(result, own_key, low, largest):
    spot = [jax.random.randint(jax.random.fold_in(own_key, axis), (), 0, length) for axis, length in enumerate(result.shape)]
    widest = result.shape.index(max(result.shape))
    neighbour = spot[:widest] + [(spot[widest] + 1) % result.shape[widest]] + spot[widest + 1:]
    return result.at[tuple(spot)].set(low).at[tuple(neighbour)].set(largest)


def levels(key, shape, shards, least, high):
    level, own = 1.0, jax.random.fold_in(key, 6)
    for position, parts in shards:
        heights = jnp.exp(jax.random.uniform(jax.random.fold_in(own, position), (parts,), jnp.float32, least / len(shards), high / len(shards)))
        level = level * jnp.repeat(heights, shape[position] // parts).reshape([-1 if axis == position else 1 for axis in range(len(shape))])
    return level


def bell_draw(rng, shape, width, limit, cuts=(), kind=jnp.bfloat16):
    values = width * jax.random.normal(rng, shape, jnp.float32)
    if cuts:
        values = values * levels(rng, shape, cuts, -0.22, 0.18)
    return jnp.clip(values, -limit, limit).astype(kind)


def setup_inputs(seed: int = 0) -> dict:
    arg_keys = jax.random.split(jax.random.key(seed), 6)
    return {
        "rhs": bell_draw(arg_keys[0], (LV, NODES, W, R), 1.0, 6.0, ((1, 64), (2, 8)), jnp.float32),
        "diag_inverse": draw_diag_inverse(jax.random.fold_in(arg_keys[5], 71), 0),
        "panels": bell_draw(arg_keys[2], (LV - 1, NODES, PB, W, W), (8 * W) ** -0.5, 0.125, ((1, 64), (3, 8))),
        "targets": draw_targets(jax.random.fold_in(arg_keys[5], 71), 0),
        "counts": with_ends(jax.random.randint(arg_keys[4], (LV - 1, NODES), 1, PB + 1), jax.random.fold_in(arg_keys[4], 1), 1, PB).astype(jnp.int32),
    }


def reference(rhs, diag_inverse, panels, targets, counts):
    residual = rhs.reshape(LV * NODES, W, R)
    solved = []
    for height in range(LV):
        pieces = residual[height * NODES:(height + 1) * NODES]
        solution = jnp.einsum("nij,njr->nir", diag_inverse[height], pieces, precision=lax.Precision.HIGHEST)
        solved.append(solution)
        if height < LV - 1:
            rounded = lax.optimization_barrier(solution.astype(jnp.bfloat16)).astype(jnp.float32)
            product = jnp.einsum("nbij,njr->nbir", panels[height].astype(jnp.float32), rounded, precision=lax.Precision.HIGHEST)
            alive_mask = (jnp.arange(PB, dtype=jnp.int32)[None, :] < counts[height][:, None]).astype(jnp.float32)
            product = product * alive_mask[:, :, None, None]
            residual = residual.at[targets[height].reshape(-1).astype(jnp.int32)].add(-product.reshape(-1, W, R))
    return jnp.stack(solved, 0)
```

```python
import jax
import jax.numpy as jnp
from jax import lax
from jax.experimental import pallas as pl
from jax.experimental.pallas import tpu as pltpu
from jax.sharding import PartitionSpec as P

MESH = pl.DeviceIdType.MESH
F32, BF16 = jnp.float32, jnp.bfloat16
TOP = 32000.0
X0, D0, S03, S01, S02, X1, D1, S11, S12, D2, S21 = range(11)
GROUPS = ((X0, D0 + 1), (S03, S02 + 1), (X1, S12 + 1), (D2, S21 + 1))
L0K1, L0K2, L0K3, L1K1, L1K2, L2K1 = 0, 1, 4, 11, 12, 15


def split(x):
    hi = x.astype(BF16)
    return hi, (x - hi.astype(F32)).astype(BF16)


def dot_nt(a, b):
    return lax.dot_general(a, b, (((1,), (1,)), ((), ())), preferred_element_type=F32)


def code(x):
    peak = jnp.maximum(jnp.max(jnp.abs(x), axis=1, keepdims=True), 1e-30)
    power = jnp.ceil(jnp.log(peak) * 1.4426950408889634 + 1e-3)
    return jnp.round(x * (jnp.exp2(-power) * TOP)), power


def to_int16(x):
    return x.astype(jnp.int32).astype(jnp.int16)


def kernel(
    rhs_ref, diag_ref, panels_ref, targets_ref, counts_ref, out_ref,
    rhs, diag, panels, coded, away, sent, came, fin, fin_in, mid, res, sol_t,
    load_sem, send_sem, recv_sem, away_sem, k_send, k_recv, fin_send, fin_recv, mid_send, mid_recv,
):
    s = lax.axis_index("snode")
    q = lax.axis_index("rowblk")
    sib = q + 1 - 2 * lax.rem(q, 2)
    sx = lax.rem(s + 32, 64)
    u2, u4, u8 = lax.rem(s, 2), lax.rem(s, 4), lax.rem(s, 8)

    loads = [
        pltpu.make_async_copy(panels_ref.at[h, 0], panels.at[h], load_sem.at[h]) for h in range(3)
    ] + [
        pltpu.make_async_copy(rhs_ref.at[:, 0], rhs, load_sem.at[3]),
        pltpu.make_async_copy(diag_ref.at[:, 0], diag, load_sem.at[4]),
    ]
    for i in (3, 4, 0, 1, 2):
        loads[i].start()

    barrier = pltpu.get_barrier_semaphore()

    def tell(node, row):
        pl.semaphore_signal(barrier, inc=1, device_id=(node, row), device_id_type=MESH)

    for i in range(1, 8):
        tell(s, lax.rem(q + i, 8))
    for i in range(8):
        tell(sx, lax.rem(q + i, 8))

    @pl.when(u2 == 0)
    def _():
        tell(s + 1, q)

    @pl.when(u4 == 0)
    def _():
        tell(s + 2, q)
        tell(s + 3, q)

    @pl.when(u8 == 0)
    def _():
        for i in range(4, 8):
            tell(s + i, q)

    lane = lax.broadcasted_iota(jnp.int32, (32, 128), 1)

    def put(slot, x, buffer, at):
        whole, power = code(x)
        if at is None:
            buffer[slot] = to_int16(whole)
        else:
            buffer[at, slot] = to_int16(whole)
        return power

    def panel_sums(h):
        kinds = 3 - h
        sums = [jnp.zeros((32, 256), F32) for _ in range(kinds)]
        for b in range(32):
            block = panels[h, b].astype(F32)
            distance = lax.shift_right_logical(targets_ref[h, b], 6) - h
            alive = b < counts_ref[h]
            for k in range(kinds):
                sums[k] = sums[k] + block * jnp.where(alive & (distance == k + 1), 1.0, 0.0)
        return sums

    def heads(first, second, powers):
        a, pa = code(first)
        b, pb = code(second)
        extra = jnp.zeros((32, 128), F32)
        for i, p in enumerate([pa, pb] + powers):
            extra = jnp.where(lane == i, p, extra)
        return to_int16(jnp.concatenate([a, b], axis=1)), to_int16(extra)

    loads[3].wait()
    loads[4].wait()
    p_d0 = put(D0, diag[0], coded, q)
    p_d2 = put(D2, diag[2], coded, q)
    p_d1 = put(D1 - X1, diag[1], away, None)
    loads[0].wait()
    s01, s02, s03 = panel_sums(0)
    p_s03 = put(S03, s03, coded, q)
    p_s01 = put(S01, s01, coded, q)
    p_s02 = put(S02, s02, coded, q)
    loads[1].wait()
    s11, s12 = panel_sums(1)
    p_s11 = put(S11 - X1, s11, away, None)
    p_s12 = put(S12 - X1, s12, away, None)
    loads[2].wait()
    (s21,) = panel_sums(2)
    p_s21 = put(S21, s21, coded, q)
    left, right = heads(rhs[0], rhs[2], [p_d0, p_s03, p_s01, p_s02, p_d2, p_s21])
    coded[q, X0, :, 0:128] = left
    coded[q, X0, :, 128:256] = right
    left, right = heads(rhs[1], rhs[3], [p_d1, p_s11, p_s12])
    away[0, :, 0:128] = left
    away[0, :, 128:256] = right

    pl.semaphore_wait(barrier, 15 + u2 + lax.rem(s // 2, 2) + lax.rem(s // 4, 2))

    def part(g, b):
        lo, hi = GROUPS[g]
        return coded.at[b, lo:hi]

    def copy(g, b, row, i):
        return pltpu.make_async_remote_copy(
            src_ref=part(g, b), dst_ref=part(g, b), send_sem=send_sem.at[g, i],
            recv_sem=recv_sem.at[g, b], device_id=(s, row), device_id_type=MESH,
        )

    def send_group(g):
        for i in range(1, 4):
            copy(g, q, lax.rem(q + 2 * i, 8), i - 1).start()
        copy(g, q, sib, 3).start()

    def forward(g):
        for i in (1, 3, 2):
            b = lax.rem(q + 2 * i, 8)
            copy(g, b, sib, 3 + i).wait_recv()
            copy(g, b, sib, 3 + i).start()

    def from_sibling(g):
        for i in range(4):
            copy(g, lax.rem(sib + 2 * i, 8), sib, 3).wait_recv()

    send_group(0)
    home = pltpu.make_async_remote_copy(
        src_ref=away, dst_ref=part(2, q), send_sem=away_sem,
        recv_sem=recv_sem.at[2, q], device_id=(sx, q), device_id_type=MESH,
    )
    home.start()
    send_group(1)
    forward(0)
    home.wait_recv()
    send_group(2)
    send_group(3)

    def matrix(m):
        return coded[:, m].reshape(256, 256).astype(jnp.int32).astype(F32)

    def apply(m, lhs, scale):
        hi, lo = split(matrix(m))
        got = dot_nt(lhs, hi) + dot_nt(lhs, lo)
        if lhs.shape[0] == 16:
            got = got[0:8] + got[8:16]
        return got * scale

    def both(x):
        hi = x.astype(BF16).astype(F32)
        return jnp.concatenate([hi, x - hi], axis=0).astype(BF16)

    pick_row = lax.broadcasted_iota(jnp.int32, (32, 256), 0)
    pick_lane = lax.broadcasted_iota(jnp.int32, (32, 256), 1)
    wanted = jnp.where(
        pick_row < 8, 8 * q + pick_row, jnp.where(pick_row < 16, 56 + 8 * q + pick_row, 112 + pick_row)
    )
    picker = jnp.where(pick_lane == wanted, 1.0, 0.0).astype(BF16)

    def read_heads(m):
        hi, lo = split(matrix(m))
        got = dot_nt(picker, hi) + dot_nt(picker, lo)
        scales = jnp.exp2(got[16:24]) * (1.0 / TOP)
        return got[0:8] * scales[0:1], got[8:16] * scales[1:2], scales

    def k_copy(kind, slot, node):
        return pltpu.make_async_remote_copy(
            src_ref=sent.at[kind], dst_ref=came.at[slot], send_sem=k_send.at[kind],
            recv_sem=k_recv.at[slot], device_id=(node, q), device_id_type=MESH,
        )

    one = lambda kind, base: k_copy(kind, base, s - 1)
    two = lambda kind, base: k_copy(kind, base + jnp.maximum(u4 - 1, 0), s - u4)
    three = lambda kind, base: k_copy(kind, base + jnp.maximum(u8 - 1, 0), s - u8)

    def push(kind, update, level, make, base, low):
        @pl.when(low == 0)
        def _():
            res[level] -= update

        @pl.when(low != 0)
        def _():
            sent[kind] = update
            make(kind, base).start()

    def pull(level, base, count, low):
        @pl.when(low == 0)
        def _():
            for i in range(count):
                k_copy(0, base + i, s).wait_recv()
                res[level] -= came[base + i]

    from_sibling(0)
    r0, r2, scales0 = read_heads(X0)
    x0 = apply(D0, both(r0), scales0[2:3]).astype(BF16)
    res[2] = r2
    forward(1)
    forward(2)
    from_sibling(2)
    r1, r3, scales1 = read_heads(X1)
    res[1] = r1
    res[3] = r3
    from_sibling(1)
    push(0, apply(S03, x0, scales0[3:4]), 3, three, L0K3, u8)
    push(1, apply(S01, x0, scales0[4:5]), 1, one, L0K1, u2)
    push(2, apply(S02, x0, scales0[5:6]), 2, two, L0K2, u4)

    pull(1, L0K1, 1, u2)
    x1 = apply(D1, both(res[1]), scales1[2:3]).astype(BF16)
    push(3, apply(S11, x1, scales1[3:4]), 2, one, L1K1, u2)
    push(4, apply(S12, x1, scales1[4:5]), 3, two, L1K2, u4)
    fin[8:16] = res[1]

    forward(3)
    from_sibling(3)
    pull(2, L0K2, 3, u4)
    pull(2, L1K1, 1, u2)
    x2 = apply(D2, both(res[2]), scales0[6:7]).astype(BF16)
    push(5, apply(S21, x2, scales0[7:8]), 3, one, L2K1, u2)

    def mid_copy(i, src, row):
        return pltpu.make_async_remote_copy(
            src_ref=res.at[2], dst_ref=mid.at[src], send_sem=mid_send.at[i],
            recv_sem=mid_recv.at[src], device_id=(s, row), device_id_type=MESH,
        )

    for i in range(1, 8):
        mid_copy(i - 1, q, lax.rem(q + i, 8)).start()
    mid[q] = res[2]

    pull(3, L1K2, 3, u4)
    pull(3, L0K3, 7, u8)
    pull(3, L2K1, 1, u2)
    fin[0:8] = res[3]

    def fin_copy(i, src, row):
        return pltpu.make_async_remote_copy(
            src_ref=fin, dst_ref=fin_in.at[src], send_sem=fin_send.at[i],
            recv_sem=fin_recv.at[src], device_id=(sx, row), device_id_type=MESH,
        )

    for i in range(8):
        fin_copy(i, q, lax.rem(q + i, 8)).start()

    def own_rows(h, columns):
        dh, dl = split(diag[h])
        ch, cl = split(columns)
        out_ref[h, 0] = dot_nt(dh, ch) + (dot_nt(dh, cl) + dot_nt(dl, ch))

    first = matrix(X0)
    start = first[:, 0:64] * (jnp.exp2(first[:, 128:129]) * (1.0 / TOP))
    dh, dl = split(diag[0])
    ch, cl = split(start)
    dot = lambda a, b: jnp.dot(a, b, preferred_element_type=F32)
    out_ref[0, 0] = dot(dh, ch) + (dot(dh, cl) + dot(dl, ch))
    for i in range(1, 8):
        mid_copy(i - 1, lax.rem(q + i, 8), q).wait_recv()
    own_rows(2, mid[...].reshape(64, 256))
    for i in range(8):
        fin_copy(i, lax.rem(q + i, 8), q).wait_recv()
    own_rows(3, fin_in[:, 0:8].reshape(64, 256))
    own_rows(1, fin_in[:, 8:16].reshape(64, 256))

    for g in range(4):
        for i in range(7):
            copy(g, q, sib, i).wait_send()
    home.wait_send()
    for i in range(7):
        mid_copy(i, q, q).wait_send()
    for i in range(8):
        fin_copy(i, q, q).wait_send()
    for kind, low in ((0, u8), (1, u2), (2, u4), (3, u2), (4, u4), (5, u2)):

        @pl.when(low != 0)
        def _(kind=kind):
            k_copy(kind, 0, s).wait_send()


def shards(rhs, diag_inverse, panels, targets, counts):
    hbm = pl.BlockSpec(memory_space=pl.ANY)
    smem = pl.BlockSpec(memory_space=pltpu.SMEM)
    dma = pltpu.SemaphoreType.DMA
    return pl.pallas_call(
        kernel,
        out_shape=jax.ShapeDtypeStruct((4, 1, 32, 64), F32),
        in_specs=[hbm, hbm, hbm, smem, smem],
        out_specs=pl.BlockSpec(memory_space=pltpu.VMEM),
        scratch_shapes=[
            pltpu.VMEM((4, 32, 64), F32),
            pltpu.VMEM((4, 32, 256), F32),
            pltpu.VMEM((3, 32, 32, 256), BF16),
            pltpu.VMEM((8, 11, 32, 256), jnp.int16),
            pltpu.VMEM((4, 32, 256), jnp.int16),
            pltpu.VMEM((6, 8, 256), F32),
            pltpu.VMEM((16, 8, 256), F32),
            pltpu.VMEM((16, 256), F32),
            pltpu.VMEM((8, 16, 256), F32),
            pltpu.VMEM((8, 8, 256), F32),
            pltpu.VMEM((4, 8, 256), F32),
            pltpu.VMEM((8, 256), F32),
            dma((5,)),
            dma((4, 7)),
            dma((4, 8)),
            dma(()),
            dma((6,)),
            dma((16,)),
            dma((8,)),
            dma((8,)),
            dma((7,)),
            dma((8,)),
        ],
        compiler_params=pltpu.CompilerParams(
            collective_id=0, has_side_effects=True, vmem_limit_bytes=24 * 1024 * 1024
        ),
        name="substitute",
    )(rhs, diag_inverse, panels, targets[:, 0], counts[:, 0])


def solution(mesh):
    in_specs = (
        P(None, "snode", "rowblk", None),
        P(None, "snode", "rowblk", None),
        P(None, "snode", None, "rowblk", None),
        P(None, "snode", None),
        P(None, "snode"),
    )
    out_specs = P(None, "snode", "rowblk", None)
    return jax.shard_map(shards, mesh=mesh, in_specs=in_specs, out_specs=out_specs, check_vma=False)
```

```python
import jax
import jax.numpy as jnp
from jax import lax
from jax.experimental import pallas as pl
from jax.experimental.pallas import tpu as pltpu
from jax.sharding import PartitionSpec as P

MESH = pl.DeviceIdType.MESH
F32, BF16 = jnp.float32, jnp.bfloat16
TOP = 32000.0
X0, D0, S03, S01, S02, X1, D1, S11, S12, D2, S21 = range(11)
GROUPS = ((X0, D0 + 1), (S03, S03 + 1), (S01, S02 + 1), (X1, S12 + 1), (D2, S21 + 1))
AWAY = 3
L0K1, L0K2, L1K1, L2HOME, L1HOME, L0HOME, SLOTS = 0, 1, 4, 5, 7, 11, 19


def split(x):
    hi = x.astype(BF16)
    return hi, (x - hi.astype(F32)).astype(BF16)


def dot_nt(a, b):
    return lax.dot_general(a, b, (((1,), (1,)), ((), ())), preferred_element_type=F32)


def code(x):
    peak = jnp.maximum(jnp.max(jnp.abs(x), axis=1, keepdims=True), 1e-30)
    power = jnp.ceil(jnp.log(peak) * 1.4426950408889634 + 1e-3)
    return jnp.round(x * (jnp.exp2(-power) * TOP)), power


def to_int16(x):
    return x.astype(jnp.int32).astype(jnp.int16)


def kernel(
    rhs_ref, diag_ref, panels_ref, targets_ref, counts_ref, out_ref,
    rhs, diag, panels, targets, counts, coded, away, sent, came, low, mid, fin, res,
    load_sem, send_sem, recv_sem, away_sem, k_send, k_recv, low_send, low_recv, mid_send, mid_recv, fin_send, fin_recv,
):
    s = lax.axis_index("snode")
    q = lax.axis_index("rowblk")
    sib = q + 1 - 2 * lax.rem(q, 2)
    sx = lax.rem(s + 32, 64)
    u2, u4, u8 = lax.rem(s, 2), lax.rem(s, 4), lax.rem(s, 8)

    loads = [
        pltpu.make_async_copy(panels_ref.at[h, 0], panels.at[h], load_sem.at[h]) for h in range(3)
    ] + [
        pltpu.make_async_copy(rhs_ref.at[:, 0], rhs, load_sem.at[3]),
        pltpu.make_async_copy(diag_ref.at[:, 0], diag, load_sem.at[4]),
        pltpu.make_async_copy(targets_ref, targets, load_sem.at[5]),
        pltpu.make_async_copy(counts_ref, counts, load_sem.at[6]),
    ]
    for i in (5, 6, 3, 4, 0, 1, 2):
        loads[i].start()

    barrier = pltpu.get_barrier_semaphore()

    def tell(node, row):
        pl.semaphore_signal(barrier, inc=1, device_id=(node, row), device_id_type=MESH)

    for i in range(1, 8):
        tell(s, lax.rem(q + i, 8))
    for i in range(8):
        tell(sx, lax.rem(q + i, 8))

    @pl.when(u2 == 0)
    def _():
        tell(s + 1, q)
        tell(sx + 1, q)

    @pl.when(u4 == 0)
    def _():
        for i in (2, 3):
            tell(s + i, q)
            tell(sx + i, q)

    @pl.when(u8 == 0)
    def _():
        for i in range(4, 8):
            tell(sx + i, q)

    lane = lax.broadcasted_iota(jnp.int32, (32, 128), 1)

    def put(slot, x, buffer, at):
        whole, power = code(x)
        if at is None:
            buffer[slot] = to_int16(whole)
        else:
            buffer[at, slot] = to_int16(whole)
        return power

    def panel_sums(h):
        kinds = 3 - h
        sums = [jnp.zeros((32, 256), F32) for _ in range(kinds)]
        for b in range(32):
            block = panels[h, b].astype(F32)
            distance = lax.shift_right_logical(targets[h, 0, b], 6) - h
            alive = b < counts[h]
            for k in range(kinds):
                sums[k] = sums[k] + block * jnp.where(alive & (distance == k + 1), 1.0, 0.0)
        return sums

    def heads(first, second, third, powers):
        parts = [code(x) for x in (first, second, third)]
        extra = jnp.zeros((32, 128), F32)
        for i, p in enumerate([power for _, power in parts] + powers):
            extra = jnp.where(lane == i, p, extra)
        left = jnp.concatenate([parts[0][0], parts[1][0]], axis=1)
        right = jnp.concatenate([extra[:, 0:64], parts[2][0]], axis=1)
        return to_int16(left), to_int16(right)

    loads[3].wait()
    loads[4].wait()
    p_d0 = put(D0, diag[0], coded, q)
    p_d2 = put(D2, diag[2], coded, q)
    p_d1 = put(D1 - X1, diag[1], away, None)
    loads[5].wait()
    loads[6].wait()
    loads[0].wait()
    s01, s02, s03 = panel_sums(0)
    p_s03 = put(S03, s03, coded, q)
    p_s01 = put(S01, s01, coded, q)
    p_s02 = put(S02, s02, coded, q)
    loads[1].wait()
    s11, s12 = panel_sums(1)
    p_s11 = put(S11 - X1, s11, away, None)
    p_s12 = put(S12 - X1, s12, away, None)
    loads[2].wait()
    (s21,) = panel_sums(2)
    p_s21 = put(S21, s21, coded, q)
    left, right = heads(rhs[0], rhs[2], rhs[3], [p_d0, p_s03, p_s01, p_s02, p_d2, p_s21])
    coded[q, X0, :, 0:128] = left
    coded[q, X0, :, 128:256] = right
    left, right = heads(rhs[1], jnp.zeros((32, 64), F32), jnp.zeros((32, 64), F32), [p_d1, p_s11, p_s12])
    away[0, :, 0:128] = left
    away[0, :, 128:256] = right

    bit1, bit2 = lax.rem(s // 2, 2), lax.rem(s // 4, 2)
    pl.semaphore_wait(barrier, 15 + 2 * (u2 + bit1) + bit2)

    def part(g, b):
        lo, hi = GROUPS[g]
        return coded.at[b, lo:hi]

    def copy(g, b, row, i):
        return pltpu.make_async_remote_copy(
            src_ref=part(g, b), dst_ref=part(g, b), send_sem=send_sem.at[g, i],
            recv_sem=recv_sem.at[g, b], device_id=(s, row), device_id_type=MESH,
        )

    def send_group(g):
        for i in range(1, 4):
            copy(g, q, lax.rem(q + 2 * i, 8), i - 1).start()
        copy(g, q, sib, 3).start()

    def forward(g):
        for i in (1, 3, 2):
            b = lax.rem(q + 2 * i, 8)
            copy(g, b, sib, 3 + i).wait_recv()
            copy(g, b, sib, 3 + i).start()

    def from_sibling(g):
        for i in range(4):
            copy(g, lax.rem(sib + 2 * i, 8), sib, 3).wait_recv()

    send_group(0)
    send_group(1)
    home = pltpu.make_async_remote_copy(
        src_ref=away, dst_ref=part(AWAY, q), send_sem=away_sem,
        recv_sem=recv_sem.at[AWAY, q], device_id=(sx, q), device_id_type=MESH,
    )
    home.start()
    send_group(2)
    forward(0)
    forward(1)
    home.wait_recv()
    send_group(AWAY)
    send_group(4)

    def matrix(m):
        return coded[:, m].reshape(256, 256).astype(jnp.int32).astype(F32)

    def apply(m, lhs, scale):
        hi, lo = split(matrix(m))
        got = dot_nt(lhs, hi) + dot_nt(lhs, lo)
        if lhs.shape[0] == 16:
            got = got[0:8] + got[8:16]
        return got * scale

    def both(x):
        hi = x.astype(BF16).astype(F32)
        return jnp.concatenate([hi, x - hi], axis=0).astype(BF16)

    pick_row = lax.broadcasted_iota(jnp.int32, (48, 256), 0)
    pick_lane = lax.broadcasted_iota(jnp.int32, (48, 256), 1)
    wanted = jnp.where(
        pick_row < 16,
        8 * q + jnp.where(pick_row < 8, pick_row, pick_row + 56),
        jnp.where(pick_row < 32, pick_row + 112, 8 * q + pick_row + 160),
    )
    picker = jnp.where(pick_lane == wanted, 1.0, 0.0).astype(BF16)

    def read_heads(m):
        hi, lo = split(matrix(m))
        got = dot_nt(picker, hi) + dot_nt(picker, lo)
        scales = jnp.exp2(got[16:32]) * (1.0 / TOP)
        rows = [got[at:at + 8] * scales[i:i + 1] for i, at in enumerate((0, 8, 32))]
        return rows, scales[3:]

    def k_copy(kind, slot, node):
        return pltpu.make_async_remote_copy(
            src_ref=sent.at[kind], dst_ref=came.at[slot], send_sem=k_send.at[kind],
            recv_sem=k_recv.at[slot], device_id=(node, q), device_id_type=MESH,
        )

    def push(kind, update, level, slot, low_bits):
        @pl.when(low_bits == 0)
        def _():
            res[level] -= update

        @pl.when(low_bits != 0)
        def _():
            sent[kind] = update
            k_copy(kind, slot + jnp.maximum(low_bits - 1, 0), s - low_bits).start()

    def push_home(kind, update, slot, low_bits):
        sent[kind] = update
        k_copy(kind, slot + low_bits, lax.rem(s - low_bits + 32, 64)).start()

    def pull(level, slot, count, low_bits):
        @pl.when(low_bits == 0)
        def _():
            for i in range(count):
                k_copy(0, slot + i, s).wait_recv()
                res[level] -= came[slot + i]

    def spread(buffer, to, sends, recvs, node, source, row, i):
        return pltpu.make_async_remote_copy(
            src_ref=buffer, dst_ref=to.at[source], send_sem=sends.at[i],
            recv_sem=recvs.at[source], device_id=(node, row), device_id_type=MESH,
        )

    low_copy = lambda i, source, row: spread(res.at[1], low, low_send, low_recv, sx, source, row, i)
    mid_copy = lambda i, source, row: spread(res.at[2], mid, mid_send, mid_recv, s, source, row, i)
    fin_copy = lambda i, source, row: spread(res.at[3], fin, fin_send, fin_recv, s, source, row, i)
    peer = lambda i: lax.rem(q + i, 8)

    res[1] = jnp.zeros((8, 256), F32)
    from_sibling(0)
    (r0, r2, r3), scales0 = read_heads(X0)
    x0 = apply(D0, both(r0), scales0[0:1]).astype(BF16)
    res[2] = r2
    res[3] = r3
    from_sibling(1)
    push_home(0, apply(S03, x0, scales0[1:2]), L0HOME, u8)
    forward(2)
    first = matrix(X0)
    start = first[:, 0:64] * (jnp.exp2(first[:, 128:129]) * (1.0 / TOP))
    dh, dl = split(diag[0])
    ch, cl = split(start)
    dot = lambda a, b: jnp.dot(a, b, preferred_element_type=F32)
    out_ref[0, 0] = dot(dh, ch) + (dot(dh, cl) + dot(dl, ch))
    from_sibling(2)
    push(1, apply(S01, x0, scales0[2:3]), 1, L0K1, u2)
    push(2, apply(S02, x0, scales0[3:4]), 2, L0K2, u4)

    forward(AWAY)
    from_sibling(AWAY)
    (r1, _, _), scales1 = read_heads(X1)
    res[1] += r1
    pull(1, L0K1, 1, u2)
    x1 = apply(D1, both(res[1]), scales1[0:1]).astype(BF16)
    push(3, apply(S11, x1, scales1[1:2]), 2, L1K1, u2)
    push_home(4, apply(S12, x1, scales1[2:3]), L1HOME, u4)
    for i in range(8):
        low_copy(i, q, peer(i)).start()

    forward(4)
    from_sibling(4)
    pull(2, L0K2, 3, u4)
    pull(2, L1K1, 1, u2)
    x2 = apply(D2, both(res[2]), scales0[4:5]).astype(BF16)
    push_home(5, apply(S21, x2, scales0[5:6]), L2HOME, u2)
    for i in range(1, 8):
        mid_copy(i - 1, q, peer(i)).start()
    mid[q] = res[2]

    pull(3, L1HOME, 4, u4)
    pull(3, L2HOME, 2, u2)
    pull(3, L0HOME, 8, u8)
    for i in range(1, 8):
        fin_copy(i - 1, q, peer(i)).start()
    fin[q] = res[3]

    def own_rows(h, columns):
        dh, dl = split(diag[h])
        ch, cl = split(columns.reshape(64, 256))
        out_ref[h, 0] = dot_nt(dh, ch) + (dot_nt(dh, cl) + dot_nt(dl, ch))

    for i in range(8):
        low_copy(i, peer(i), q).wait_recv()
    own_rows(1, low[...])
    for i in range(1, 8):
        mid_copy(i - 1, peer(i), q).wait_recv()
    own_rows(2, mid[...])
    for i in range(1, 8):
        fin_copy(i - 1, peer(i), q).wait_recv()
    own_rows(3, fin[...])

    for g in range(5):
        for i in range(7):
            copy(g, q, sib, i).wait_send()
    home.wait_send()
    for i in range(8):
        low_copy(i, q, q).wait_send()
    for i in range(7):
        mid_copy(i, q, q).wait_send()
        fin_copy(i, q, q).wait_send()
    for kind in (0, 4, 5):
        k_copy(kind, 0, s).wait_send()
    for kind, low_bits in ((1, u2), (2, u4), (3, u2)):

        @pl.when(low_bits != 0)
        def _(kind=kind):
            k_copy(kind, 0, s).wait_send()


def shards(rhs, diag_inverse, panels, targets, counts):
    hbm = pl.BlockSpec(memory_space=pltpu.HBM)
    dma = pltpu.SemaphoreType.DMA
    return pl.pallas_call(
        kernel,
        out_shape=pltpu.VMEM((4, 1, 32, 64), F32),
        in_specs=[hbm] * 5,
        out_specs=pl.BlockSpec(memory_space=pltpu.VMEM),
        scratch_shapes=[
            pltpu.VMEM((4, 32, 64), F32),
            pltpu.VMEM((4, 32, 256), F32),
            pltpu.VMEM((3, 32, 32, 256), BF16),
            pltpu.SMEM((3, 1, 32), jnp.int32),
            pltpu.SMEM((3,), jnp.int32),
            pltpu.VMEM((8, 11, 32, 256), jnp.int16),
            pltpu.VMEM((4, 32, 256), jnp.int16),
            pltpu.VMEM((6, 8, 256), F32),
            pltpu.VMEM((SLOTS, 8, 256), F32),
            pltpu.VMEM((8, 8, 256), F32),
            pltpu.VMEM((8, 8, 256), F32),
            pltpu.VMEM((8, 8, 256), F32),
            pltpu.VMEM((4, 8, 256), F32),
            dma((7,)),
            dma((5, 7)),
            dma((5, 8)),
            dma(()),
            dma((6,)),
            dma((SLOTS,)),
            dma((8,)),
            dma((8,)),
            dma((7,)),
            dma((8,)),
            dma((7,)),
            dma((8,)),
        ],
        compiler_params=pltpu.CompilerParams(
            collective_id=0, has_side_effects=True, vmem_limit_bytes=62 * 1024 * 1024
        ),
        name="substitute",
    )(rhs, diag_inverse, panels, targets, counts[:, 0])


def solution(mesh):
    in_specs = (
        P(None, "snode", "rowblk", None),
        P(None, "snode", "rowblk", None),
        P(None, "snode", None, "rowblk", None),
        P(None, "snode", None),
        P(None, "snode"),
    )
    out_specs = P(None, "snode", "rowblk", None)
    return jax.shard_map(shards, mesh=mesh, in_specs=in_specs, out_specs=out_specs, check_vma=False)
```

```python
import jax
import jax.numpy as jnp
from jax import lax
from jax.experimental import pallas as pl
from jax.experimental.pallas import tpu as pltpu
from jax.sharding import PartitionSpec as P

MESH = pl.DeviceIdType.MESH
F32, BF16 = jnp.float32, jnp.bfloat16
TOP = 32000.0
S03, S01, S02, X1, D1, S11, S12, X2, D2, S21 = range(10)
GROUPS = ((0, 0), (S03, S03 + 1), (S01, S02 + 1), (X1, S12 + 1), (X2, S21 + 1))
AWAY = 3
L0K1, L0K2, L1K1, L2HOME, L1HOME, L0HOME, SLOTS = 0, 1, 4, 5, 7, 11, 19


def split(x):
    hi = x.astype(BF16)
    return hi, (x - hi.astype(F32)).astype(BF16)


def dot_nt(a, b):
    return lax.dot_general(a, b, (((1,), (1,)), ((), ())), preferred_element_type=F32)


def code(x):
    peak = jnp.maximum(jnp.max(jnp.abs(x), axis=1, keepdims=True), 1e-30)
    power = jnp.ceil(jnp.log(peak) * 1.4426950408889634 + 1e-3)
    return jnp.round(x * (jnp.exp2(-power) * TOP)), power


def to_int16(x):
    return x.astype(jnp.int32).astype(jnp.int16)


def kernel(
    rhs_ref, diag_ref, panels_ref, targets_ref, counts_ref, out_ref,
    rhs, diag, panels, targets, counts, coded, away, first, sent, came, pair, mid, fin, res,
    load_sem, send_sem, recv_sem, away_sem, k_send, k_recv, low_send, low_recv, mid_send, mid_recv, fin_send, fin_recv, chain,
):
    s = lax.axis_index("snode")
    q = lax.axis_index("rowblk")
    sib = q + 1 - 2 * lax.rem(q, 2)
    sx = lax.rem(s + 32, 64)
    u2, u4, u8 = lax.rem(s, 2), lax.rem(s, 4), lax.rem(s, 8)

    loads = [
        pltpu.make_async_copy(panels_ref.at[h, 0], panels.at[h], load_sem.at[h]) for h in range(3)
    ] + [
        pltpu.make_async_copy(rhs_ref.at[:, 0], rhs, load_sem.at[3]),
        pltpu.make_async_copy(diag_ref.at[:, 0], diag, load_sem.at[4]),
        pltpu.make_async_copy(targets_ref, targets, load_sem.at[5]),
        pltpu.make_async_copy(counts_ref, counts, load_sem.at[6]),
    ]
    for i in (5, 6, 3, 4, 0, 1, 2):
        loads[i].start()

    barrier = pltpu.get_barrier_semaphore()

    def tell(node, row):
        pl.semaphore_signal(barrier, inc=1, device_id=(node, row), device_id_type=MESH)

    for i in (4, 3, 5, 2, 6, 7, 1):
        tell(s, lax.rem(q + i, 8))
    tell(sx, q)

    @pl.when(u8 != 0)
    def _():
        tell(s - 1, q)

    def hand_on(step):
        @pl.when(step & (u8 != 0))
        def _():
            pl.semaphore_wait(chain, 1)

        @pl.when(step & (u8 != 7))
        def _():
            pl.semaphore_signal(chain, inc=1, device_id=(s + 1, q), device_id_type=MESH)


    def put(slot, x, buffer, at):
        whole, power = code(x)
        if at is None:
            buffer[slot] = to_int16(whole)
        else:
            buffer[at, slot] = to_int16(whole)
        return power

    def panel_sums(h):
        kinds = 3 - h
        sums = [jnp.zeros((32, 256), F32) for _ in range(kinds)]
        for b in range(32):
            block = panels[h, b].astype(F32)
            distance = lax.shift_right_logical(targets[h, 0, b], 6) - h
            alive = b < counts[h]
            for k in range(kinds):
                sums[k] = sums[k] + block * jnp.where(alive & (distance == k + 1), 1.0, 0.0)
        return sums

    def scales_of(powers, width, at):
        extra = jnp.zeros((32, width), F32)
        where = lax.broadcasted_iota(jnp.int32, (32, width), 1)
        for i, p in enumerate(powers):
            extra = jnp.where(where == at + i, p, extra)
        return extra

    def wide_heads(buffer, at, left, right, powers):
        buffer[(*at, slice(None), slice(0, 128))] = to_int16(jnp.concatenate([left, right], axis=1))
        buffer[(*at, slice(None), slice(128, 256))] = to_int16(scales_of(powers, 128, 0))

    loads[3].wait()
    loads[4].wait()
    d0_code, p_d0 = code(diag[0])
    r0_code, p_r0 = code(rhs[0])
    loads[5].wait()
    loads[6].wait()
    loads[0].wait()
    s01, s02, s03 = panel_sums(0)
    p_s03 = put(S03, s03, coded, q)
    p_s01 = put(S01, s01, coded, q)
    p_s02 = put(S02, s02, coded, q)
    scales = scales_of([p_r0, p_d0, p_s03, p_s01, p_s02], 64, 0)
    first[q, 0:32] = to_int16(d0_code)
    heads0 = to_int16(jnp.concatenate([r0_code, scales], axis=1))
    first[q, 32:48, 0:128] = heads0[0:16]
    first[q, 32:48, 128:256] = heads0[16:32]
    res[1] = jnp.zeros((8, 256), F32)
    res[2] = jnp.zeros((8, 256), F32)

    pl.semaphore_wait(barrier, jnp.where(u8 == 7, 8, 9))

    def part(g, b):
        lo, hi = GROUPS[g]
        return coded.at[b, lo:hi] if hi else first.at[b]

    def copy(g, b, row, i):
        return pltpu.make_async_remote_copy(
            src_ref=part(g, b), dst_ref=part(g, b), send_sem=send_sem.at[g, i],
            recv_sem=recv_sem.at[g, b], device_id=(s, row), device_id_type=MESH,
        )

    def send_group(g):
        for i in range(1, 4):
            copy(g, q, lax.rem(q + 2 * i, 8), i - 1).start()
        copy(g, q, sib, 3).start()

    def forward(g):
        for i in (1, 3, 2):
            b = lax.rem(q + 2 * i, 8)
            copy(g, b, sib, 3 + i).wait_recv()
            copy(g, b, sib, 3 + i).start()

    def from_sibling(g):
        for i in range(4):
            copy(g, lax.rem(sib + 2 * i, 8), sib, 3).wait_recv()

    peer = lambda i: lax.rem(q + i, 8)

    def spread(buffer, to, sends, recvs, source, row, i):
        return pltpu.make_async_remote_copy(
            src_ref=buffer, dst_ref=to.at[source], send_sem=sends.at[i],
            recv_sem=recvs.at[source], device_id=(s, row), device_id_type=MESH,
        )

    mid_copy = lambda i, source, row: spread(pair, mid, mid_send, mid_recv, source, row, i)
    fin_copy = lambda i, source, row: spread(res.at[3], fin, fin_send, fin_recv, source, row, i)

    send_group(0)
    send_group(1)
    hand_on(u8 == 0)
    p_d1 = put(D1 - X1, diag[1], away, None)
    r1_code, p_r1 = code(rhs[1])
    loads[1].wait()
    s11, s12 = panel_sums(1)
    p_s11 = put(S11 - X1, s11, away, None)
    p_s12 = put(S12 - X1, s12, away, None)
    wide_heads(away, (0,), r1_code, jnp.zeros((32, 64), F32), [p_r1, p_d1, p_s11, p_s12])
    home = pltpu.make_async_remote_copy(
        src_ref=away, dst_ref=part(AWAY, q), send_sem=away_sem,
        recv_sem=recv_sem.at[AWAY, q], device_id=(sx, q), device_id_type=MESH,
    )
    home.start()
    send_group(2)
    p_d2 = put(D2, diag[2], coded, q)
    r2_code, p_r2 = code(rhs[2])
    r3_code, p_r3 = code(rhs[3])
    loads[2].wait()
    (s21,) = panel_sums(2)
    p_s21 = put(S21, s21, coded, q)
    wide_heads(coded, (q, X2), r2_code, r3_code, [p_r2, p_r3, p_d2, p_s21])
    hand_on((u8 > 0) & (u8 < 5))
    forward(0)
    forward(1)
    home.wait_recv()
    send_group(AWAY)
    send_group(4)
    hand_on(u8 == 5)

    def whole(x):
        return x.reshape(256, x.shape[2]).astype(jnp.int32).astype(F32)

    def matrix(m):
        return whole(coded[:, m])

    def apply(numbers, lhs, scale):
        hi, lo = split(numbers)
        got = dot_nt(lhs, hi) + dot_nt(lhs, lo)
        if lhs.shape[0] == 16:
            got = got[0:8] + got[8:16]
        return got * scale

    def both(x):
        hi = x.astype(BF16).astype(F32)
        return jnp.concatenate([hi, x - hi], axis=0).astype(BF16)

    def read_heads(x, at):
        row = lax.broadcasted_iota(jnp.int32, (32, x.shape[1]), 0)
        pick_lane = lax.broadcasted_iota(jnp.int32, (32, x.shape[1]), 1)
        wanted = jnp.where(row < 16, 8 * q + jnp.where(row < 8, row, row + 56), row - 16 + at)
        picker = jnp.where(pick_lane == wanted, 1.0, 0.0).astype(BF16)
        hi, lo = split(x)
        got = dot_nt(picker, hi) + dot_nt(picker, lo)
        return got[0:8], got[8:16], jnp.exp2(got[16:32]) * (1.0 / TOP)

    def k_copy(kind, slot, node):
        return pltpu.make_async_remote_copy(
            src_ref=sent.at[kind], dst_ref=came.at[slot], send_sem=k_send.at[kind],
            recv_sem=k_recv.at[slot], device_id=(node, q), device_id_type=MESH,
        )

    def push(kind, update, level, slot, low_bits):
        @pl.when(low_bits == 0)
        def _():
            res[level] -= update

        @pl.when(low_bits != 0)
        def _():
            sent[kind] = update
            k_copy(kind, slot + jnp.maximum(low_bits - 1, 0), s - low_bits).start()

    def push_home(kind, update, slot, low_bits):
        sent[kind] = update
        k_copy(kind, slot + low_bits, lax.rem(s - low_bits + 32, 64)).start()

    def pull(level, slot, count, low_bits):
        @pl.when(low_bits == 0)
        def _():
            for i in range(count):
                k_copy(0, slot + i, s).wait_recv()
                res[level] -= came[slot + i]

    from_sibling(0)
    whole0 = whole(jnp.concatenate([first[:, 32:48, 0:128], first[:, 32:48, 128:256]], axis=1))
    r0, _, scales0 = read_heads(whole0, 64)
    lhs0 = both(r0 * scales0[0:1])
    x0 = apply(whole(first[:, 0:32]), lhs0, scales0[1:2]).astype(BF16)
    from_sibling(1)
    hand_on(u8 > 5)
    push_home(0, apply(matrix(S03), x0, scales0[2:3]), L0HOME, u8)
    forward(2)
    start = whole0[:, 0:64] * (jnp.exp2(whole0[:, 64:65]) * (1.0 / TOP))
    dh, dl = split(diag[0])
    ch, cl = split(start)
    dot = lambda a, b: jnp.dot(a, b, preferred_element_type=F32)
    out_ref[0, 0] = dot(dh, ch) + (dot(dh, cl) + dot(dl, ch))
    from_sibling(2)
    push(1, apply(matrix(S01), x0, scales0[3:4]), 1, L0K1, u2)
    push(2, apply(matrix(S02), x0, scales0[4:5]), 2, L0K2, u4)

    forward(AWAY)
    from_sibling(AWAY)
    forward(4)
    r1, _, scales1 = read_heads(matrix(X1), 128)
    res[1] += r1 * scales1[0:1]
    pull(1, L0K1, 1, u2)
    x1 = apply(matrix(D1), both(res[1]), scales1[1:2]).astype(BF16)
    push(3, apply(matrix(S11), x1, scales1[2:3]), 2, L1K1, u2)
    push_home(4, apply(matrix(S12), x1, scales1[3:4]), L1HOME, u4)
    back = pltpu.make_async_remote_copy(
        src_ref=res.at[1], dst_ref=pair.at[1], send_sem=low_send, recv_sem=low_recv,
        device_id=(sx, q), device_id_type=MESH,
    )
    back.start()

    from_sibling(4)
    r2, r3, scales2 = read_heads(matrix(X2), 128)
    res[2] += r2 * scales2[0:1]
    res[3] = r3 * scales2[1:2]
    pull(2, L0K2, 3, u4)
    pull(2, L1K1, 1, u2)
    x2 = apply(matrix(D2), both(res[2]), scales2[2:3]).astype(BF16)
    push_home(5, apply(matrix(S21), x2, scales2[3:4]), L2HOME, u2)
    pair[0] = res[2]
    back.wait_recv()
    for i in range(1, 8):
        mid_copy(i - 1, q, peer(i)).start()
    mid[q] = pair[...]

    pull(3, L1HOME, 4, u4)
    pull(3, L2HOME, 2, u2)
    pull(3, L0HOME, 8, u8)
    for i in (4, 3, 5, 2, 6, 7, 1):
        fin_copy(i - 1, q, peer(i)).start()
    fin[q] = res[3]

    def own_rows(h, columns):
        dh, dl = split(diag[h])
        ch, cl = split(columns.reshape(64, 256))
        out_ref[h, 0] = dot_nt(dh, ch) + (dot_nt(dh, cl) + dot_nt(dl, ch))

    for i in range(1, 8):
        mid_copy(i - 1, peer(i), q).wait_recv()
    own_rows(1, mid[:, 1])
    own_rows(2, mid[:, 0])
    for i in range(1, 8):
        fin_copy(i - 1, peer(i), q).wait_recv()
    own_rows(3, fin[...])

    for g in range(5):
        for i in range(7):
            copy(g, q, sib, i).wait_send()
    home.wait_send()
    back.wait_send()
    for i in range(7):
        mid_copy(i, q, q).wait_send()
        fin_copy(i, q, q).wait_send()
    for kind in (0, 4, 5):
        k_copy(kind, 0, s).wait_send()
    for kind, low_bits in ((1, u2), (2, u4), (3, u2)):

        @pl.when(low_bits != 0)
        def _(kind=kind):
            k_copy(kind, 0, s).wait_send()


def shards(rhs, diag_inverse, panels, targets, counts):
    hbm = pl.BlockSpec(memory_space=pltpu.HBM)
    dma = pltpu.SemaphoreType.DMA
    return pl.pallas_call(
        kernel,
        out_shape=pltpu.VMEM((4, 1, 32, 64), F32),
        in_specs=[hbm] * 5,
        out_specs=pl.BlockSpec(memory_space=pltpu.VMEM),
        scratch_shapes=[
            pltpu.VMEM((4, 32, 64), F32),
            pltpu.VMEM((4, 32, 256), F32),
            pltpu.VMEM((3, 32, 32, 256), BF16),
            pltpu.SMEM((3, 1, 32), jnp.int32),
            pltpu.SMEM((3,), jnp.int32),
            pltpu.VMEM((8, 10, 32, 256), jnp.int16),
            pltpu.VMEM((4, 32, 256), jnp.int16),
            pltpu.VMEM((8, 48, 256), jnp.int16),
            pltpu.VMEM((6, 8, 256), F32),
            pltpu.VMEM((SLOTS, 8, 256), F32),
            pltpu.VMEM((2, 8, 256), F32),
            pltpu.VMEM((8, 2, 8, 256), F32),
            pltpu.VMEM((8, 8, 256), F32),
            pltpu.VMEM((4, 8, 256), F32),
            dma((7,)),
            dma((5, 7)),
            dma((5, 8)),
            dma(()),
            dma((6,)),
            dma((SLOTS,)),
            dma(()),
            dma(()),
            dma((7,)),
            dma((8,)),
            dma((7,)),
            dma((8,)),
            pltpu.SemaphoreType.REGULAR,
        ],
        compiler_params=pltpu.CompilerParams(
            collective_id=0, has_side_effects=True, vmem_limit_bytes=62 * 1024 * 1024
        ),
        name="substitute",
    )(rhs, diag_inverse, panels, targets, counts[:, 0])


def solution(mesh):
    in_specs = (
        P(None, "snode", "rowblk", None),
        P(None, "snode", "rowblk", None),
        P(None, "snode", None, "rowblk", None),
        P(None, "snode", None),
        P(None, "snode"),
    )
    out_specs = P(None, "snode", "rowblk", None)
    return jax.shard_map(shards, mesh=mesh, in_specs=in_specs, out_specs=out_specs, check_vma=False)
```

```python
import jax
import jax.numpy as jnp
from jax import lax
from jax.experimental import pallas as pl
from jax.experimental.pallas import tpu as pltpu
from jax.sharding import PartitionSpec as P

MESH = pl.DeviceIdType.MESH
F32, BF16 = jnp.float32, jnp.bfloat16
TOP = 32000.0
S03, S01, S02, X1, D1, S11, S12, X2, D2, S21 = range(10)
GROUPS = ((0, 0), (S03, S03 + 1), (S01, S02 + 1), (X1, D1 + 1), (S11, S12 + 1), (X2, S21 + 1))
AWAY = 3
L0K1, L0K2, L1K1, L2HOME, L1HOME, L0HOME, SLOTS = 0, 1, 4, 5, 7, 11, 19


def split(x):
    hi = x.astype(BF16)
    return hi, (x - hi.astype(F32)).astype(BF16)


def dot_nt(a, b):
    return lax.dot_general(a, b, (((1,), (1,)), ((), ())), preferred_element_type=F32)


def code(x):
    peak = jnp.maximum(jnp.max(jnp.abs(x), axis=1, keepdims=True), 1e-30)
    power = jnp.ceil(jnp.log(peak) * 1.4426950408889634 + 1e-3)
    return jnp.round(x * (jnp.exp2(-power) * TOP)), power


def to_int16(x):
    return x.astype(jnp.int32).astype(jnp.int16)


def kernel(
    rhs_ref, diag_ref, panels_ref, targets_ref, counts_ref, out_ref,
    rhs, diag, panels, targets, counts, coded, away, first, sent, came, pair, mid, fin, res,
    load_sem, send_sem, near_recv, sib_recv, away_sem, home_recv, k_send, k_recv, low_recv,
    mid_send, mid_recv, fin_send, fin_recv, chain,
):
    s = lax.axis_index("snode")
    q = lax.axis_index("rowblk")
    sib = q + 1 - 2 * lax.rem(q, 2)
    sx = lax.rem(s + 32, 64)
    u2, u4, u8 = lax.rem(s, 2), lax.rem(s, 4), lax.rem(s, 8)

    loads = [
        pltpu.make_async_copy(panels_ref.at[h, 0], panels.at[h], load_sem.at[h]) for h in range(3)
    ] + [
        pltpu.make_async_copy(rhs_ref.at[:, 0], rhs, load_sem.at[3]),
        pltpu.make_async_copy(diag_ref.at[:, 0], diag, load_sem.at[4]),
        pltpu.make_async_copy(targets_ref, targets, load_sem.at[5]),
        pltpu.make_async_copy(counts_ref, counts, load_sem.at[6]),
    ]
    for i in (5, 6, 3, 4, 0, 1, 2):
        loads[i].start()

    barrier = pltpu.get_barrier_semaphore()

    def tell(node, row):
        pl.semaphore_signal(barrier, inc=1, device_id=(node, row), device_id_type=MESH)

    for i in (4, 3, 5, 2, 6, 7, 1):
        tell(s, lax.rem(q + i, 8))
    tell(sx, q)

    @pl.when(u8 != 0)
    def _():
        tell(s - 1, q)

    def hand_on(step):
        @pl.when(step & (u8 != 0))
        def _():
            pl.semaphore_wait(chain, 1)

        @pl.when(step & (u8 != 7))
        def _():
            pl.semaphore_signal(chain, inc=1, device_id=(s + 1, q), device_id_type=MESH)


    def put(slot, x, buffer, at):
        whole, power = code(x)
        if at is None:
            buffer[slot] = to_int16(whole)
        else:
            buffer[at, slot] = to_int16(whole)
        return power

    def panel_sums(h):
        kinds = 3 - h
        sums = [jnp.zeros((32, 256), F32) for _ in range(kinds)]
        for b in range(32):
            block = panels[h, b].astype(F32)
            distance = lax.shift_right_logical(targets[h, 0, b], 6) - h
            alive = b < counts[h]
            for k in range(kinds):
                sums[k] = sums[k] + block * jnp.where(alive & (distance == k + 1), 1.0, 0.0)
        return sums

    def scales_of(powers, width, at):
        extra = jnp.zeros((32, width), F32)
        where = lax.broadcasted_iota(jnp.int32, (32, width), 1)
        for i, p in enumerate(powers):
            extra = jnp.where(where == at + i, p, extra)
        return extra

    def wide_heads(buffer, at, left, right, powers):
        buffer[(*at, slice(None), slice(0, 128))] = to_int16(jnp.concatenate([left, right], axis=1))
        buffer[(*at, slice(None), slice(128, 256))] = to_int16(scales_of(powers, 128, 0))

    loads[3].wait()
    loads[4].wait()
    d0_code, p_d0 = code(diag[0])
    r0_code, p_r0 = code(rhs[0])
    loads[5].wait()
    loads[6].wait()
    loads[0].wait()
    s01, s02, s03 = panel_sums(0)
    p_s03 = put(S03, s03, coded, q)
    p_s01 = put(S01, s01, coded, q)
    p_s02 = put(S02, s02, coded, q)
    scales = scales_of([p_r0, p_d0, p_s03, p_s01, p_s02], 64, 0)
    first[q, 0:32] = to_int16(d0_code)
    heads0 = to_int16(jnp.concatenate([r0_code, scales], axis=1))
    first[q, 32:48, 0:128] = heads0[0:16]
    first[q, 32:48, 128:256] = heads0[16:32]
    res[1] = jnp.zeros((8, 256), F32)
    res[2] = jnp.zeros((8, 256), F32)

    pl.semaphore_wait(barrier, jnp.where(u8 == 7, 8, 9))

    def part(g, b):
        lo, hi = GROUPS[g]
        return coded.at[b, lo:hi] if hi else first.at[b]

    def blocks(g, n):
        lo, hi = GROUPS[g]
        return coded.at[0:n, lo:hi] if hi else first.at[0:n]

    def total(view, sem):
        return pltpu.make_async_remote_copy(
            src_ref=view, dst_ref=view, send_sem=sem, recv_sem=sem,
            device_id=(s, sib), device_id_type=MESH,
        )

    def copy(g, b, row, recv):
        return pltpu.make_async_remote_copy(
            src_ref=part(g, b), dst_ref=part(g, b), send_sem=send_sem.at[g],
            recv_sem=recv, device_id=(s, row), device_id_type=MESH,
        )

    near = lambda g, i: near_recv.at[i - 1 if g == 0 else g + 2]

    def send_group(g):
        for i in range(1, 4):
            copy(g, q, lax.rem(q + 2 * i, 8), near(g, i)).start()
        copy(g, q, sib, sib_recv.at[g]).start()

    def forward(g):
        if g:
            total(blocks(g, 3), near(g, 1)).wait_recv()
        for i in (1, 3, 2):
            b = lax.rem(q + 8 - 2 * i, 8)
            if g == 0:
                copy(g, b, sib, near(g, i)).wait_recv()
            copy(g, b, sib, sib_recv.at[g]).start()

    def from_sibling(g):
        total(blocks(g, 4), sib_recv.at[g]).wait_recv()

    peer = lambda i: lax.rem(q + i, 8)

    def spread(buffer, to, send, recv, row):
        return pltpu.make_async_remote_copy(
            src_ref=buffer, dst_ref=to.at[q], send_sem=send,
            recv_sem=recv, device_id=(s, row), device_id_type=MESH,
        )

    mid_copy = lambda row: spread(pair, mid, mid_send, mid_recv, row)
    fin_copy = lambda row: spread(res.at[3], fin, fin_send, fin_recv, row)

    send_group(0)
    send_group(1)
    hand_on(u8 == 0)
    p_d1 = put(D1 - X1, diag[1], away, None)
    r1_code, p_r1 = code(rhs[1])
    loads[1].wait()
    s11, s12 = panel_sums(1)
    p_s11 = put(S11 - X1, s11, away, None)
    p_s12 = put(S12 - X1, s12, away, None)
    wide_heads(away, (0,), r1_code, jnp.zeros((32, 64), F32), [p_r1, p_d1, p_s11, p_s12])
    moves = [
        pltpu.make_async_remote_copy(
            src_ref=away.at[2 * i:2 * i + 2], dst_ref=part(AWAY + i, q), send_sem=away_sem,
            recv_sem=home_recv.at[i], device_id=(sx, q), device_id_type=MESH,
        )
        for i in range(2)
    ]
    for move in moves:
        move.start()
    send_group(2)
    p_d2 = put(D2, diag[2], coded, q)
    r2_code, p_r2 = code(rhs[2])
    r3_code, p_r3 = code(rhs[3])
    loads[2].wait()
    (s21,) = panel_sums(2)
    p_s21 = put(S21, s21, coded, q)
    wide_heads(coded, (q, X2), r2_code, r3_code, [p_r2, p_r3, p_d2, p_s21])
    hand_on((u8 > 0) & (u8 < 5))
    forward(0)
    forward(1)
    for i, move in enumerate(moves):
        move.wait_recv()
        send_group(AWAY + i)
    send_group(5)
    hand_on(u8 == 5)

    def whole(x):
        return x.reshape(256, x.shape[2]).astype(jnp.int32).astype(F32)

    def matrix(m):
        return whole(coded[:, m])

    def apply(numbers, lhs, scale):
        hi, lo = split(numbers)
        got = dot_nt(lhs, hi) + dot_nt(lhs, lo)
        if lhs.shape[0] == 16:
            got = got[0:8] + got[8:16]
        return got * scale

    def both(x):
        hi = x.astype(BF16).astype(F32)
        return jnp.concatenate([hi, x - hi], axis=0).astype(BF16)

    def read_heads(x, at):
        row = lax.broadcasted_iota(jnp.int32, (32, x.shape[1]), 0)
        pick_lane = lax.broadcasted_iota(jnp.int32, (32, x.shape[1]), 1)
        wanted = jnp.where(row < 16, 8 * q + jnp.where(row < 8, row, row + 56), row - 16 + at)
        picker = jnp.where(pick_lane == wanted, 1.0, 0.0).astype(BF16)
        hi, lo = split(x)
        got = dot_nt(picker, hi) + dot_nt(picker, lo)
        return got[0:8], got[8:16], jnp.exp2(got[16:32]) * (1.0 / TOP)

    family = {L0K1: 0, L0K2: 1, L1K1: 2, L2HOME: 3, L1HOME: 4, L0HOME: 5}
    sharing = (0, 1, 2, 1, 0, 0)

    def k_copy(kind, first_slot, offset, node):
        return pltpu.make_async_remote_copy(
            src_ref=sent.at[kind], dst_ref=came.at[first_slot + offset], send_sem=k_send.at[sharing[kind]],
            recv_sem=k_recv.at[family[first_slot]], device_id=(node, q), device_id_type=MESH,
        )

    def push(kind, update, level, slot, low_bits):
        @pl.when(low_bits == 0)
        def _():
            res[level] -= update

        @pl.when(low_bits != 0)
        def _():
            sent[kind] = update
            k_copy(kind, slot, jnp.maximum(low_bits - 1, 0), s - low_bits).start()

    def push_home(kind, update, slot, low_bits):
        sent[kind] = update
        k_copy(kind, slot, low_bits, lax.rem(s - low_bits + 32, 64)).start()

    def pull(level, slot, count, low_bits):
        @pl.when(low_bits == 0)
        def _():
            total(came.at[slot:slot + count], k_recv.at[family[slot]]).wait_recv()
            for i in range(count):
                res[level] -= came[slot + i]

    from_sibling(0)
    whole0 = whole(jnp.concatenate([first[:, 32:48, 0:128], first[:, 32:48, 128:256]], axis=1))
    r0, _, scales0 = read_heads(whole0, 64)
    lhs0 = both(r0 * scales0[0:1])
    x0 = apply(whole(first[:, 0:32]), lhs0, scales0[1:2]).astype(BF16)
    from_sibling(1)
    hand_on(u8 > 5)
    push_home(0, apply(matrix(S03), x0, scales0[2:3]), L0HOME, u8)
    forward(2)
    start = whole0[:, 0:64] * (jnp.exp2(whole0[:, 64:65]) * (1.0 / TOP))
    dh, dl = split(diag[0])
    ch, cl = split(start)
    dot = lambda a, b: jnp.dot(a, b, preferred_element_type=F32)
    out_ref[0, 0] = dot(dh, ch) + (dot(dh, cl) + dot(dl, ch))
    from_sibling(2)
    push(1, apply(matrix(S01), x0, scales0[3:4]), 1, L0K1, u2)
    push(2, apply(matrix(S02), x0, scales0[4:5]), 2, L0K2, u4)

    forward(AWAY)
    forward(AWAY + 1)
    from_sibling(AWAY)
    r1, _, scales1 = read_heads(matrix(X1), 128)
    res[1] += r1 * scales1[0:1]
    pull(1, L0K1, 1, u2)
    x1 = apply(matrix(D1), both(res[1]), scales1[1:2]).astype(BF16)
    from_sibling(AWAY + 1)
    push(3, apply(matrix(S11), x1, scales1[2:3]), 2, L1K1, u2)
    push_home(4, apply(matrix(S12), x1, scales1[3:4]), L1HOME, u4)
    back = pltpu.make_async_remote_copy(
        src_ref=res.at[1], dst_ref=pair.at[1], send_sem=k_send.at[0], recv_sem=low_recv,
        device_id=(sx, q), device_id_type=MESH,
    )
    back.start()
    forward(5)
    from_sibling(5)
    r2, r3, scales2 = read_heads(matrix(X2), 128)
    res[2] += r2 * scales2[0:1]
    res[3] = r3 * scales2[1:2]
    pull(2, L0K2, 3, u4)
    pull(2, L1K1, 1, u2)
    x2 = apply(matrix(D2), both(res[2]), scales2[2:3]).astype(BF16)
    push_home(5, apply(matrix(S21), x2, scales2[3:4]), L2HOME, u2)
    pair[0] = res[2]
    back.wait_recv()
    for i in range(1, 8):
        mid_copy(peer(i)).start()
    mid[q] = pair[...]

    pull(3, L1HOME, 4, u4)
    pull(3, L2HOME, 2, u2)
    pull(3, L0HOME, 8, u8)
    for i in (4, 3, 5, 2, 6, 7, 1):
        fin_copy(peer(i)).start()
    fin[q] = res[3]

    def own_rows(h, columns):
        dh, dl = split(diag[h])
        ch, cl = split(columns.reshape(64, 256))
        out_ref[h, 0] = dot_nt(dh, ch) + (dot_nt(dh, cl) + dot_nt(dl, ch))

    total(mid.at[0:7], mid_recv).wait_recv()
    own_rows(1, mid[:, 1])
    own_rows(2, mid[:, 0])
    total(fin.at[0:7], fin_recv).wait_recv()
    own_rows(3, fin[...])

    for g in range(6):
        total(blocks(g, 7), send_sem.at[g]).wait_send()
    total(away, away_sem).wait_send()
    total(mid.at[0:7], mid_send).wait_send()
    total(fin.at[0:7], fin_send).wait_send()
    total(sent.at[0:4], k_send.at[0]).wait_send()

    @pl.when(u2 != 0)
    def _():
        total(sent.at[0:2], k_send.at[1]).wait_send()

    @pl.when(u4 != 0)
    def _():
        total(sent.at[0:1], k_send.at[2]).wait_send()


def shards(rhs, diag_inverse, panels, targets, counts):
    hbm = pl.BlockSpec(memory_space=pltpu.HBM)
    dma = pltpu.SemaphoreType.DMA
    return pl.pallas_call(
        kernel,
        out_shape=pltpu.VMEM((4, 1, 32, 64), F32),
        in_specs=[hbm] * 5,
        out_specs=pl.BlockSpec(memory_space=pltpu.VMEM),
        scratch_shapes=[
            pltpu.VMEM((4, 32, 64), F32),
            pltpu.VMEM((4, 32, 256), F32),
            pltpu.VMEM((3, 32, 32, 256), BF16),
            pltpu.SMEM((3, 1, 32), jnp.int32),
            pltpu.SMEM((3,), jnp.int32),
            pltpu.VMEM((8, 10, 32, 256), jnp.int16),
            pltpu.VMEM((4, 32, 256), jnp.int16),
            pltpu.VMEM((8, 48, 256), jnp.int16),
            pltpu.VMEM((6, 8, 256), F32),
            pltpu.VMEM((SLOTS, 8, 256), F32),
            pltpu.VMEM((2, 8, 256), F32),
            pltpu.VMEM((8, 2, 8, 256), F32),
            pltpu.VMEM((8, 8, 256), F32),
            pltpu.VMEM((4, 8, 256), F32),
            dma((7,)),
            dma((6,)),
            dma((8,)),
            dma((6,)),
            dma(()),
            dma((2,)),
            dma((3,)),
            dma((6,)),
            dma(()),
            dma(()),
            dma(()),
            dma(()),
            dma(()),
            pltpu.SemaphoreType.REGULAR,
        ],
        compiler_params=pltpu.CompilerParams(
            collective_id=0, has_side_effects=True, vmem_limit_bytes=62 * 1024 * 1024
        ),
        name="substitute",
    )(rhs, diag_inverse, panels, targets, counts[:, 0])


def solution(mesh):
    in_specs = (
        P(None, "snode", "rowblk", None),
        P(None, "snode", "rowblk", None),
        P(None, "snode", None, "rowblk", None),
        P(None, "snode", None),
        P(None, "snode"),
    )
    out_specs = P(None, "snode", "rowblk", None)
    return jax.shard_map(shards, mesh=mesh, in_specs=in_specs, out_specs=out_specs, check_vma=False)
```

```python
import jax
import jax.numpy as jnp
from jax import lax
from jax.experimental import pallas as pl
from jax.experimental.pallas import tpu as pltpu
from jax.sharding import PartitionSpec as P

MESH = pl.DeviceIdType.MESH
F32, BF16 = jnp.float32, jnp.bfloat16
TOP = 32000.0
S03, S01, S02, X1, D1, S11, S12, X2, D2, S21 = range(10)
GROUPS = ((0, 0), (S03, S03 + 1), (S01, S02 + 1), (X1, D1 + 1), (S11, S12 + 1), (X2, S21 + 1))
AWAY = 3
L0K1, L0K2, L1K1, L2HOME, L1HOME, L0HOME, SLOTS = 0, 1, 4, 5, 7, 11, 19


def split(x):
    hi = x.astype(BF16)
    return hi, (x - hi.astype(F32)).astype(BF16)


def dot_nt(a, b):
    return lax.dot_general(a, b, (((1,), (1,)), ((), ())), preferred_element_type=F32)


def code(x):
    peak = jnp.maximum(jnp.max(jnp.abs(x), axis=1, keepdims=True), 1e-30)
    power = jnp.ceil(jnp.log(peak) * 1.4426950408889634 + 1e-3)
    return jnp.round(x * (jnp.exp2(-power) * TOP)), power


def to_int16(x):
    return x.astype(jnp.int32).astype(jnp.int16)


def kernel(
    rhs_ref, diag_ref, panels_ref, targets_ref, counts_ref, out_ref,
    rhs, diag, panels, targets, counts, coded, away, first, sent, came, pair, mid, fin, res,
    load_sem, send_sem, near_recv, sib_recv, home_recv, k_recv, low_recv, mid_recv, fin_recv, chain,
):
    s = lax.axis_index("snode")
    q = lax.axis_index("rowblk")
    sib = q + 1 - 2 * lax.rem(q, 2)
    sx = lax.rem(s + 32, 64)
    u2, u4, u8 = lax.rem(s, 2), lax.rem(s, 4), lax.rem(s, 8)

    loads = [
        pltpu.make_async_copy(panels_ref.at[h, 0], panels.at[h], load_sem.at[h]) for h in range(3)
    ] + [
        pltpu.make_async_copy(rhs_ref.at[:, 0], rhs, load_sem.at[3]),
        pltpu.make_async_copy(diag_ref.at[:, 0], diag, load_sem.at[4]),
        pltpu.make_async_copy(targets_ref, targets, load_sem.at[5]),
        pltpu.make_async_copy(counts_ref, counts, load_sem.at[6]),
    ]
    for i in (5, 6, 3, 4, 0, 1, 2):
        loads[i].start()

    barrier = pltpu.get_barrier_semaphore()

    def tell(node, row):
        pl.semaphore_signal(barrier, inc=1, device_id=(node, row), device_id_type=MESH)

    for i in (4, 3, 5, 2, 6, 7, 1):
        tell(s, lax.rem(q + i, 8))
    tell(sx, q)

    @pl.when(u8 != 0)
    def _():
        tell(s - 1, q)

    def hand_on(step):
        @pl.when(step & (u8 != 0))
        def _():
            pl.semaphore_wait(chain, 1)

        @pl.when(step & (u8 != 7))
        def _():
            pl.semaphore_signal(chain, inc=1, device_id=(s + 1, q), device_id_type=MESH)


    def put(slot, x, buffer, at):
        whole, power = code(x)
        if at is None:
            buffer[slot] = to_int16(whole)
        else:
            buffer[at, slot] = to_int16(whole)
        return power

    def panel_sums(h):
        kinds = 3 - h
        sums = [jnp.zeros((32, 256), F32) for _ in range(kinds)]
        for b in range(32):
            block = panels[h, b].astype(F32)
            distance = lax.shift_right_logical(targets[h, 0, b], 6) - h
            alive = b < counts[h]
            for k in range(kinds):
                sums[k] = sums[k] + block * jnp.where(alive & (distance == k + 1), 1.0, 0.0)
        return sums

    def scales_of(powers, width, at):
        extra = jnp.zeros((32, width), F32)
        where = lax.broadcasted_iota(jnp.int32, (32, width), 1)
        for i, p in enumerate(powers):
            extra = jnp.where(where == at + i, p, extra)
        return extra

    def wide_heads(buffer, at, left, right, powers):
        buffer[(*at, slice(None), slice(0, 128))] = to_int16(jnp.concatenate([left, right], axis=1))
        buffer[(*at, slice(None), slice(128, 256))] = to_int16(scales_of(powers, 128, 0))

    loads[3].wait()
    loads[4].wait()
    d0_code, p_d0 = code(diag[0])
    r0_code, p_r0 = code(rhs[0])
    loads[5].wait()
    loads[6].wait()
    loads[0].wait()
    s01, s02, s03 = panel_sums(0)
    p_s03 = put(S03, s03, coded, q)
    p_s01 = put(S01, s01, coded, q)
    p_s02 = put(S02, s02, coded, q)
    scales = scales_of([p_r0, p_d0, p_s03, p_s01, p_s02], 64, 0)
    first[q, 0:32] = to_int16(d0_code)
    heads0 = to_int16(jnp.concatenate([r0_code, scales], axis=1))
    first[q, 32:48, 0:128] = heads0[0:16]
    first[q, 32:48, 128:256] = heads0[16:32]
    res[1] = jnp.zeros((8, 256), F32)
    res[2] = jnp.zeros((8, 256), F32)

    pl.semaphore_wait(barrier, jnp.where(u8 == 7, 8, 9))

    def part(g, b):
        lo, hi = GROUPS[g]
        return coded.at[b, lo:hi] if hi else first.at[b]

    def blocks(g, n):
        lo, hi = GROUPS[g]
        return coded.at[0:n, lo:hi] if hi else first.at[0:n]

    def total(view, sem):
        return pltpu.make_async_remote_copy(
            src_ref=view, dst_ref=view, send_sem=sem, recv_sem=sem,
            device_id=(s, sib), device_id_type=MESH,
        )

    def copy(g, b, row, recv):
        return pltpu.make_async_remote_copy(
            src_ref=part(g, b), dst_ref=part(g, b), send_sem=send_sem.at[1 if g == 0 else 0],
            recv_sem=recv, device_id=(s, row), device_id_type=MESH,
        )

    near = lambda g, i: near_recv.at[i - 1 if g == 0 else g + 2]

    def send_group(g):
        for i in range(1, 4):
            copy(g, q, lax.rem(q + 2 * i, 8), near(g, i)).start()
        copy(g, q, sib, sib_recv.at[g]).start()

    def forward(g):
        if g:
            total(blocks(g, 3), near(g, 1)).wait_recv()
        for i in (1, 3, 2):
            b = lax.rem(q + 8 - 2 * i, 8)
            if g == 0:
                copy(g, b, sib, near(g, i)).wait_recv()
            copy(g, b, sib, sib_recv.at[g]).start()

    def from_sibling(g):
        total(blocks(g, 4), sib_recv.at[g]).wait_recv()

    peer = lambda i: lax.rem(q + i, 8)

    def spread(buffer, to, send, recv, row):
        return pltpu.make_async_remote_copy(
            src_ref=buffer, dst_ref=to.at[q], send_sem=send,
            recv_sem=recv, device_id=(s, row), device_id_type=MESH,
        )

    mid_copy = lambda row: spread(pair, mid, send_sem.at[1], mid_recv, row)
    fin_copy = lambda row: spread(res.at[3], fin, send_sem.at[1], fin_recv, row)

    send_group(0)
    send_group(1)
    hand_on(u8 == 0)
    p_d1 = put(D1 - X1, diag[1], away, None)
    r1_code, p_r1 = code(rhs[1])
    loads[1].wait()
    s11, s12 = panel_sums(1)
    p_s11 = put(S11 - X1, s11, away, None)
    p_s12 = put(S12 - X1, s12, away, None)
    wide_heads(away, (0,), r1_code, jnp.zeros((32, 64), F32), [p_r1, p_d1, p_s11, p_s12])
    moves = [
        pltpu.make_async_remote_copy(
            src_ref=away.at[2 * i:2 * i + 2], dst_ref=part(AWAY + i, q), send_sem=send_sem.at[1],
            recv_sem=home_recv.at[i], device_id=(sx, q), device_id_type=MESH,
        )
        for i in range(2)
    ]
    for move in moves:
        move.start()
    send_group(2)
    p_d2 = put(D2, diag[2], coded, q)
    r2_code, p_r2 = code(rhs[2])
    r3_code, p_r3 = code(rhs[3])
    loads[2].wait()
    (s21,) = panel_sums(2)
    p_s21 = put(S21, s21, coded, q)
    wide_heads(coded, (q, X2), r2_code, r3_code, [p_r2, p_r3, p_d2, p_s21])
    hand_on((u8 > 0) & (u8 < 5))
    forward(0)
    forward(1)
    for i, move in enumerate(moves):
        move.wait_recv()
        send_group(AWAY + i)
    send_group(5)
    hand_on((u8 == 5) | (u8 == 6))

    def whole(x):
        return x.reshape(256, x.shape[2]).astype(jnp.int32).astype(F32)

    def matrix(m):
        return whole(coded[:, m])

    def apply(numbers, lhs, scale):
        hi, lo = split(numbers)
        got = dot_nt(lhs, hi) + dot_nt(lhs, lo)
        if lhs.shape[0] == 16:
            got = got[0:8] + got[8:16]
        return got * scale

    def both(x):
        hi = x.astype(BF16).astype(F32)
        return jnp.concatenate([hi, x - hi], axis=0).astype(BF16)

    def read_heads(x, at):
        row = lax.broadcasted_iota(jnp.int32, (32, x.shape[1]), 0)
        pick_lane = lax.broadcasted_iota(jnp.int32, (32, x.shape[1]), 1)
        wanted = jnp.where(row < 16, 8 * q + jnp.where(row < 8, row, row + 56), row - 16 + at)
        picker = jnp.where(pick_lane == wanted, 1.0, 0.0).astype(BF16)
        hi, lo = split(x)
        got = dot_nt(picker, hi) + dot_nt(picker, lo)
        return got[0:8], got[8:16], jnp.exp2(got[16:32]) * (1.0 / TOP)

    family = {L0K1: 0, L0K2: 1, L1K1: 2, L2HOME: 3, L1HOME: 4, L0HOME: 5}
    sharing = (1, 2, 3, 2, 1, 1)

    def k_copy(kind, first_slot, offset, node):
        return pltpu.make_async_remote_copy(
            src_ref=sent.at[kind], dst_ref=came.at[first_slot + offset], send_sem=send_sem.at[sharing[kind]],
            recv_sem=k_recv.at[family[first_slot]], device_id=(node, q), device_id_type=MESH,
        )

    def push(kind, update, level, slot, low_bits):
        @pl.when(low_bits == 0)
        def _():
            res[level] -= update

        @pl.when(low_bits != 0)
        def _():
            sent[kind] = update
            k_copy(kind, slot, jnp.maximum(low_bits - 1, 0), s - low_bits).start()

    def push_home(kind, update, slot, low_bits):
        sent[kind] = update
        k_copy(kind, slot, low_bits, lax.rem(s - low_bits + 32, 64)).start()

    def pull(level, slot, count, low_bits):
        @pl.when(low_bits == 0)
        def _():
            total(came.at[slot:slot + count], k_recv.at[family[slot]]).wait_recv()
            for i in range(count):
                res[level] -= came[slot + i]

    from_sibling(0)
    whole0 = whole(jnp.concatenate([first[:, 32:48, 0:128], first[:, 32:48, 128:256]], axis=1))
    r0, _, scales0 = read_heads(whole0, 64)
    lhs0 = both(r0 * scales0[0:1])
    x0 = apply(whole(first[:, 0:32]), lhs0, scales0[1:2]).astype(BF16)
    from_sibling(1)
    hand_on(u8 == 7)
    push_home(0, apply(matrix(S03), x0, scales0[2:3]), L0HOME, u8)
    forward(2)
    start = whole0[:, 0:64] * (jnp.exp2(whole0[:, 64:65]) * (1.0 / TOP))
    dh, dl = split(diag[0])
    ch, cl = split(start)
    dot = lambda a, b: jnp.dot(a, b, preferred_element_type=F32)
    out_ref[0, 0] = dot(dh, ch) + (dot(dh, cl) + dot(dl, ch))
    from_sibling(2)
    push(1, apply(matrix(S01), x0, scales0[3:4]), 1, L0K1, u2)
    push(2, apply(matrix(S02), x0, scales0[4:5]), 2, L0K2, u4)

    forward(AWAY)
    forward(AWAY + 1)
    from_sibling(AWAY)
    r1, _, scales1 = read_heads(matrix(X1), 128)
    res[1] += r1 * scales1[0:1]
    pull(1, L0K1, 1, u2)
    x1 = apply(matrix(D1), both(res[1]), scales1[1:2]).astype(BF16)
    from_sibling(AWAY + 1)
    push(3, apply(matrix(S11), x1, scales1[2:3]), 2, L1K1, u2)
    push_home(4, apply(matrix(S12), x1, scales1[3:4]), L1HOME, u4)
    back = pltpu.make_async_remote_copy(
        src_ref=res.at[1], dst_ref=pair.at[1], send_sem=send_sem.at[1], recv_sem=low_recv,
        device_id=(sx, q), device_id_type=MESH,
    )
    back.start()
    forward(5)
    from_sibling(5)
    r2, r3, scales2 = read_heads(matrix(X2), 128)
    res[2] += r2 * scales2[0:1]
    res[3] = r3 * scales2[1:2]
    pull(2, L0K2, 3, u4)
    pull(2, L1K1, 1, u2)
    x2 = apply(matrix(D2), both(res[2]), scales2[2:3]).astype(BF16)
    push_home(5, apply(matrix(S21), x2, scales2[3:4]), L2HOME, u2)
    pair[0] = res[2]
    back.wait_recv()
    for i in range(1, 8):
        mid_copy(peer(i)).start()
    mid[q] = pair[...]

    pull(3, L1HOME, 4, u4)
    pull(3, L2HOME, 2, u2)
    pull(3, L0HOME, 8, u8)
    for i in (4, 3, 5, 2, 6, 7, 1):
        fin_copy(peer(i)).start()
    fin[q] = res[3]

    def own_rows(h, columns):
        dh, dl = split(diag[h])
        ch, cl = split(columns.reshape(64, 256))
        out_ref[h, 0] = dot_nt(dh, ch) + (dot_nt(dh, cl) + dot_nt(dl, ch))

    total(mid.at[0:7], mid_recv).wait_recv()
    own_rows(1, mid[:, 1])
    own_rows(2, mid[:, 0])
    total(fin.at[0:7], fin_recv).wait_recv()
    own_rows(3, fin[...])

    total(coded.at[0:7], send_sem.at[0]).wait_send()
    total(coded.at[0:3, 0:9], send_sem.at[1]).wait_send()

    @pl.when(u2 != 0)
    def _():
        total(sent.at[0:2], send_sem.at[2]).wait_send()

    @pl.when(u4 != 0)
    def _():
        total(sent.at[0:1], send_sem.at[3]).wait_send()


def shards(rhs, diag_inverse, panels, targets, counts):
    hbm = pl.BlockSpec(memory_space=pltpu.HBM)
    dma = pltpu.SemaphoreType.DMA
    return pl.pallas_call(
        kernel,
        out_shape=pltpu.VMEM((4, 1, 32, 64), F32),
        in_specs=[hbm] * 5,
        out_specs=pl.BlockSpec(memory_space=pltpu.VMEM),
        scratch_shapes=[
            pltpu.VMEM((4, 32, 64), F32),
            pltpu.VMEM((4, 32, 256), F32),
            pltpu.VMEM((3, 32, 32, 256), BF16),
            pltpu.SMEM((3, 1, 32), jnp.int32),
            pltpu.SMEM((3,), jnp.int32),
            pltpu.VMEM((8, 10, 32, 256), jnp.int16),
            pltpu.VMEM((4, 32, 256), jnp.int16),
            pltpu.VMEM((8, 48, 256), jnp.int16),
            pltpu.VMEM((6, 8, 256), F32),
            pltpu.VMEM((SLOTS, 8, 256), F32),
            pltpu.VMEM((2, 8, 256), F32),
            pltpu.VMEM((8, 2, 8, 256), F32),
            pltpu.VMEM((8, 8, 256), F32),
            pltpu.VMEM((4, 8, 256), F32),
            dma((7,)),
            dma((4,)),
            dma((8,)),
            dma((6,)),
            dma((2,)),
            dma((6,)),
            dma(()),
            dma(()),
            dma(()),
            pltpu.SemaphoreType.REGULAR,
        ],
        compiler_params=pltpu.CompilerParams(
            collective_id=0, has_side_effects=True, vmem_limit_bytes=62 * 1024 * 1024
        ),
        name="substitute",
    )(rhs, diag_inverse, panels, targets, counts[:, 0])


def solution(mesh):
    in_specs = (
        P(None, "snode", "rowblk", None),
        P(None, "snode", "rowblk", None),
        P(None, "snode", None, "rowblk", None),
        P(None, "snode", None),
        P(None, "snode"),
    )
    out_specs = P(None, "snode", "rowblk", None)
    return jax.shard_map(shards, mesh=mesh, in_specs=in_specs, out_specs=out_specs, check_vma=False)
```

```python
import jax
import jax.numpy as jnp
from jax import lax
from jax.experimental import pallas as pl
from jax.experimental.pallas import tpu as pltpu
from jax.sharding import PartitionSpec as P

MESH = pl.DeviceIdType.MESH
F32, BF16 = jnp.float32, jnp.bfloat16
TOP = 32000.0
S03, S01, S02, X1, D1, S11, S12, X2, D2, S21 = range(10)
GROUPS = ((0, 0), (S03, S03 + 1), (S01, S02 + 1), (X1, D1 + 1), (S11, S12 + 1), (X2, S21 + 1))
AWAY = 3
L0K1, L0K2, L1K1, L2HOME, L1HOME, L0HOME, SLOTS = 0, 1, 4, 5, 7, 11, 19


def split(x):
    hi = x.astype(BF16)
    return hi, (x - hi.astype(F32)).astype(BF16)


def dot_nt(a, b):
    return lax.dot_general(a, b, (((1,), (1,)), ((), ())), preferred_element_type=F32)


def code(x):
    peak = jnp.maximum(jnp.max(jnp.abs(x), axis=1, keepdims=True), 1e-30)
    power = jnp.ceil(jnp.log(peak) * 1.4426950408889634 + 1e-3)
    return jnp.round(x * (jnp.exp2(-power) * TOP)), power


def to_int16(x):
    return x.astype(jnp.int32).astype(jnp.int16)


def kernel(
    rhs_ref, diag_ref, panels_ref, targets_ref, counts_ref, out_ref,
    rhs, diag, panels, targets, counts, coded, away, first, sent, came, pair, mid, fin, res,
    load_sem, send_sem, near_recv, sib_recv, home_recv, k_recv, low_recv, mid_recv, fin_recv, chain,
):
    s = lax.axis_index("snode")
    q = lax.axis_index("rowblk")
    sib = q + 1 - 2 * lax.rem(q, 2)
    sx = lax.rem(s + 32, 64)
    u2, u4, u8 = lax.rem(s, 2), lax.rem(s, 4), lax.rem(s, 8)

    loads = [
        pltpu.make_async_copy(panels_ref.at[h, 0], panels.at[h], load_sem.at[h]) for h in range(3)
    ] + [
        pltpu.make_async_copy(rhs_ref.at[:, 0], rhs, load_sem.at[3]),
        pltpu.make_async_copy(diag_ref.at[:, 0], diag, load_sem.at[4]),
        pltpu.make_async_copy(targets_ref, targets, load_sem.at[5]),
        pltpu.make_async_copy(counts_ref, counts, load_sem.at[6]),
    ]
    for i in (5, 6, 3, 4, 0, 1, 2):
        loads[i].start()

    barrier = pltpu.get_barrier_semaphore()

    def tell(node, row):
        pl.semaphore_signal(barrier, inc=1, device_id=(node, row), device_id_type=MESH)

    for i in (4, 3, 5, 2, 6, 7, 1):
        tell(s, lax.rem(q + i, 8))
    tell(sx, q)

    @pl.when(u8 != 0)
    def _():
        tell(s - 1, q)

    def hand_on(step):
        @pl.when(step & (u8 != 0))
        def _():
            pl.semaphore_wait(chain, 1)

        @pl.when(step & (u8 != 7))
        def _():
            pl.semaphore_signal(chain, inc=1, device_id=(s + 1, q), device_id_type=MESH)


    def put(slot, x, buffer, at):
        whole, power = code(x)
        if at is None:
            buffer[slot] = to_int16(whole)
        else:
            buffer[at, slot] = to_int16(whole)
        return power

    def panel_sums(h):
        kinds = 3 - h
        sums = [jnp.zeros((32, 256), F32) for _ in range(kinds)]
        for b in range(32):
            block = panels[h, b].astype(F32)
            distance = lax.shift_right_logical(targets[h, 0, b], 6) - h
            alive = b < counts[h]
            for k in range(kinds):
                sums[k] = sums[k] + block * jnp.where(alive & (distance == k + 1), 1.0, 0.0)
        return sums

    def scales_of(powers, width, at):
        extra = jnp.zeros((32, width), F32)
        where = lax.broadcasted_iota(jnp.int32, (32, width), 1)
        for i, p in enumerate(powers):
            extra = jnp.where(where == at + i, p, extra)
        return extra

    def wide_heads(buffer, at, left, right, powers):
        buffer[(*at, slice(None), slice(0, 128))] = to_int16(jnp.concatenate([left, right], axis=1))
        buffer[(*at, slice(None), slice(128, 256))] = to_int16(scales_of(powers, 128, 0))

    loads[3].wait()
    loads[4].wait()
    d0_code, p_d0 = code(diag[0])
    r0_code, p_r0 = code(rhs[0])
    loads[5].wait()
    loads[6].wait()
    loads[0].wait()
    s01, s02, s03 = panel_sums(0)
    p_s03 = put(S03, s03, coded, q)
    p_s01 = put(S01, s01, coded, q)
    p_s02 = put(S02, s02, coded, q)
    scales = scales_of([p_r0, p_d0, p_s03, p_s01, p_s02], 64, 0)
    first[q, 0:32] = to_int16(d0_code)
    heads0 = to_int16(jnp.concatenate([r0_code, scales], axis=1))
    first[q, 32:48, 0:128] = heads0[0:16]
    first[q, 32:48, 128:256] = heads0[16:32]
    res[1] = jnp.zeros((8, 256), F32)
    res[2] = jnp.zeros((8, 256), F32)

    pl.semaphore_wait(barrier, jnp.where(u8 == 7, 8, 9))

    def part(g, b):
        lo, hi = GROUPS[g]
        return coded.at[b, lo:hi] if hi else first.at[b]

    def blocks(g, n):
        lo, hi = GROUPS[g]
        return coded.at[0:n, lo:hi] if hi else first.at[0:n]

    def total(view, sem):
        return pltpu.make_async_remote_copy(
            src_ref=view, dst_ref=view, send_sem=sem, recv_sem=sem,
            device_id=(s, sib), device_id_type=MESH,
        )

    def copy(g, b, row, recv):
        return pltpu.make_async_remote_copy(
            src_ref=part(g, b), dst_ref=part(g, b), send_sem=send_sem.at[1 if g == 0 else 0],
            recv_sem=recv, device_id=(s, row), device_id_type=MESH,
        )

    near = lambda g, i: near_recv.at[i - 1 if g == 0 else g + 2]

    def send_group(g):
        for i in range(1, 4):
            copy(g, q, lax.rem(q + 2 * i, 8), near(g, i)).start()
        copy(g, q, sib, sib_recv.at[g]).start()

    def forward(g):
        if g:
            total(blocks(g, 3), near(g, 1)).wait_recv()
        for i in (1, 3, 2):
            b = lax.rem(q + 8 - 2 * i, 8)
            if g == 0:
                copy(g, b, sib, near(g, i)).wait_recv()
            copy(g, b, sib, sib_recv.at[g]).start()

    def from_sibling(g):
        total(blocks(g, 4), sib_recv.at[g]).wait_recv()

    peer = lambda i: lax.rem(q + i, 8)

    def spread(buffer, to, send, recv, row):
        return pltpu.make_async_remote_copy(
            src_ref=buffer, dst_ref=to.at[q], send_sem=send,
            recv_sem=recv, device_id=(s, row), device_id_type=MESH,
        )

    mid_copy = lambda row: spread(pair, mid, send_sem.at[1], mid_recv, row)
    fin_copy = lambda row: spread(res.at[3], fin, send_sem.at[1], fin_recv, row)

    send_group(0)
    send_group(1)
    hand_on(u8 == 0)
    p_d1 = put(D1 - X1, diag[1], away, None)
    r1_code, p_r1 = code(rhs[1])
    loads[1].wait()
    s11, s12 = panel_sums(1)
    p_s11 = put(S11 - X1, s11, away, None)
    p_s12 = put(S12 - X1, s12, away, None)
    wide_heads(away, (0,), r1_code, jnp.zeros((32, 64), F32), [p_r1, p_d1, p_s11, p_s12])
    moves = [
        pltpu.make_async_remote_copy(
            src_ref=away.at[2 * i:2 * i + 2], dst_ref=part(AWAY + i, q), send_sem=send_sem.at[1],
            recv_sem=home_recv.at[i], device_id=(sx, q), device_id_type=MESH,
        )
        for i in range(2)
    ]
    for move in moves:
        move.start()
    send_group(2)
    p_d2 = put(D2, diag[2], coded, q)
    r2_code, p_r2 = code(rhs[2])
    r3_code, p_r3 = code(rhs[3])
    loads[2].wait()
    (s21,) = panel_sums(2)
    p_s21 = put(S21, s21, coded, q)
    wide_heads(coded, (q, X2), r2_code, r3_code, [p_r2, p_r3, p_d2, p_s21])
    hand_on((u8 > 0) & (u8 < 5))
    forward(0)
    @pl.when(lax.rem(q, 2) == 1)
    def _():
        forward(1)

    for i, move in enumerate(moves):
        move.wait_recv()
        send_group(AWAY + i)
    send_group(5)
    hand_on((u8 == 5) | (u8 == 6))

    def whole(x):
        return x.reshape(256, x.shape[2]).astype(jnp.int32).astype(F32)

    def matrix(m):
        return whole(coded[:, m])

    def apply(numbers, lhs, scale):
        hi, lo = split(numbers)
        got = dot_nt(lhs, hi) + dot_nt(lhs, lo)
        if lhs.shape[0] == 16:
            got = got[0:8] + got[8:16]
        return got * scale

    def both(x):
        hi = x.astype(BF16).astype(F32)
        return jnp.concatenate([hi, x - hi], axis=0).astype(BF16)

    def read_heads(x, at):
        row = lax.broadcasted_iota(jnp.int32, (32, x.shape[1]), 0)
        pick_lane = lax.broadcasted_iota(jnp.int32, (32, x.shape[1]), 1)
        wanted = jnp.where(row < 16, 8 * q + jnp.where(row < 8, row, row + 56), row - 16 + at)
        picker = jnp.where(pick_lane == wanted, 1.0, 0.0).astype(BF16)
        hi, lo = split(x)
        got = dot_nt(picker, hi) + dot_nt(picker, lo)
        return got[0:8], got[8:16], jnp.exp2(got[16:32]) * (1.0 / TOP)

    family = {L0K1: 0, L0K2: 1, L1K1: 2, L2HOME: 3, L1HOME: 4, L0HOME: 5}
    sharing = (1, 2, 3, 2, 1, 1)

    def k_copy(kind, first_slot, offset, node):
        return pltpu.make_async_remote_copy(
            src_ref=sent.at[kind], dst_ref=came.at[first_slot + offset], send_sem=send_sem.at[sharing[kind]],
            recv_sem=k_recv.at[family[first_slot]], device_id=(node, q), device_id_type=MESH,
        )

    def push(kind, update, level, slot, low_bits):
        @pl.when(low_bits == 0)
        def _():
            res[level] -= update

        @pl.when(low_bits != 0)
        def _():
            sent[kind] = update
            k_copy(kind, slot, jnp.maximum(low_bits - 1, 0), s - low_bits).start()

    def push_home(kind, update, slot, low_bits):
        sent[kind] = update
        k_copy(kind, slot, low_bits, lax.rem(s - low_bits + 32, 64)).start()

    def pull(level, slot, count, low_bits):
        @pl.when(low_bits == 0)
        def _():
            total(came.at[slot:slot + count], k_recv.at[family[slot]]).wait_recv()
            for i in range(count):
                res[level] -= came[slot + i]

    from_sibling(0)
    whole0 = whole(jnp.concatenate([first[:, 32:48, 0:128], first[:, 32:48, 128:256]], axis=1))
    r0, _, scales0 = read_heads(whole0, 64)
    lhs0 = both(r0 * scales0[0:1])
    x0 = apply(whole(first[:, 0:32]), lhs0, scales0[1:2]).astype(BF16)
    @pl.when(lax.rem(q, 2) == 0)
    def _():
        forward(1)

    from_sibling(1)
    hand_on(u8 == 7)
    push_home(0, apply(matrix(S03), x0, scales0[2:3]), L0HOME, u8)
    forward(2)
    start = whole0[:, 0:64] * (jnp.exp2(whole0[:, 64:65]) * (1.0 / TOP))
    dh, dl = split(diag[0])
    ch, cl = split(start)
    dot = lambda a, b: jnp.dot(a, b, preferred_element_type=F32)
    out_ref[0, 0] = dot(dh, ch) + (dot(dh, cl) + dot(dl, ch))
    from_sibling(2)
    push(1, apply(matrix(S01), x0, scales0[3:4]), 1, L0K1, u2)
    push(2, apply(matrix(S02), x0, scales0[4:5]), 2, L0K2, u4)

    forward(AWAY)
    forward(AWAY + 1)
    from_sibling(AWAY)
    r1, _, scales1 = read_heads(matrix(X1), 128)
    res[1] += r1 * scales1[0:1]
    pull(1, L0K1, 1, u2)
    x1 = apply(matrix(D1), both(res[1]), scales1[1:2]).astype(BF16)
    from_sibling(AWAY + 1)
    push(3, apply(matrix(S11), x1, scales1[2:3]), 2, L1K1, u2)
    push_home(4, apply(matrix(S12), x1, scales1[3:4]), L1HOME, u4)
    back = pltpu.make_async_remote_copy(
        src_ref=res.at[1], dst_ref=pair.at[1], send_sem=send_sem.at[1], recv_sem=low_recv,
        device_id=(sx, q), device_id_type=MESH,
    )
    back.start()
    forward(5)
    from_sibling(5)
    r2, r3, scales2 = read_heads(matrix(X2), 128)
    res[2] += r2 * scales2[0:1]
    res[3] = r3 * scales2[1:2]
    pull(2, L0K2, 3, u4)
    pull(2, L1K1, 1, u2)
    x2 = apply(matrix(D2), both(res[2]), scales2[2:3]).astype(BF16)
    push_home(5, apply(matrix(S21), x2, scales2[3:4]), L2HOME, u2)
    pair[0] = res[2]
    back.wait_recv()
    for i in range(1, 8):
        mid_copy(peer(i)).start()
    mid[q] = pair[...]

    pull(3, L1HOME, 4, u4)
    pull(3, L2HOME, 2, u2)
    pull(3, L0HOME, 8, u8)
    for i in (4, 3, 5, 2, 6, 7, 1):
        fin_copy(peer(i)).start()
    fin[q] = res[3]

    def own_rows(h, columns):
        dh, dl = split(diag[h])
        ch, cl = split(columns.reshape(64, 256))
        out_ref[h, 0] = dot_nt(dh, ch) + (dot_nt(dh, cl) + dot_nt(dl, ch))

    total(mid.at[0:7], mid_recv).wait_recv()
    own_rows(1, mid[:, 1])
    own_rows(2, mid[:, 0])
    total(fin.at[0:7], fin_recv).wait_recv()
    own_rows(3, fin[...])

    total(coded.at[0:7], send_sem.at[0]).wait_send()
    total(coded.at[0:3, 0:9], send_sem.at[1]).wait_send()

    @pl.when(u2 != 0)
    def _():
        total(sent.at[0:2], send_sem.at[2]).wait_send()

    @pl.when(u4 != 0)
    def _():
        total(sent.at[0:1], send_sem.at[3]).wait_send()


def shards(rhs, diag_inverse, panels, targets, counts):
    hbm = pl.BlockSpec(memory_space=pltpu.HBM)
    dma = pltpu.SemaphoreType.DMA
    return pl.pallas_call(
        kernel,
        out_shape=pltpu.VMEM((4, 1, 32, 64), F32),
        in_specs=[hbm] * 5,
        out_specs=pl.BlockSpec(memory_space=pltpu.VMEM),
        scratch_shapes=[
            pltpu.VMEM((4, 32, 64), F32),
            pltpu.VMEM((4, 32, 256), F32),
            pltpu.VMEM((3, 32, 32, 256), BF16),
            pltpu.SMEM((3, 1, 32), jnp.int32),
            pltpu.SMEM((3,), jnp.int32),
            pltpu.VMEM((8, 10, 32, 256), jnp.int16),
            pltpu.VMEM((4, 32, 256), jnp.int16),
            pltpu.VMEM((8, 48, 256), jnp.int16),
            pltpu.VMEM((6, 8, 256), F32),
            pltpu.VMEM((SLOTS, 8, 256), F32),
            pltpu.VMEM((2, 8, 256), F32),
            pltpu.VMEM((8, 2, 8, 256), F32),
            pltpu.VMEM((8, 8, 256), F32),
            pltpu.VMEM((4, 8, 256), F32),
            dma((7,)),
            dma((4,)),
            dma((8,)),
            dma((6,)),
            dma((2,)),
            dma((6,)),
            dma(()),
            dma(()),
            dma(()),
            pltpu.SemaphoreType.REGULAR,
        ],
        compiler_params=pltpu.CompilerParams(
            collective_id=0, has_side_effects=True, vmem_limit_bytes=62 * 1024 * 1024
        ),
        name="substitute",
    )(rhs, diag_inverse, panels, targets, counts[:, 0])


def solution(mesh):
    in_specs = (
        P(None, "snode", "rowblk", None),
        P(None, "snode", "rowblk", None),
        P(None, "snode", None, "rowblk", None),
        P(None, "snode", None),
        P(None, "snode"),
    )
    out_specs = P(None, "snode", "rowblk", None)
    return jax.shard_map(shards, mesh=mesh, in_specs=in_specs, out_specs=out_specs, check_vma=False)
```

```python
import jax
import jax.numpy as jnp
from jax import lax
from jax.experimental import pallas as pl
from jax.experimental.pallas import tpu as pltpu
from jax.sharding import PartitionSpec as P

MESH = pl.DeviceIdType.MESH
F32, BF16 = jnp.float32, jnp.bfloat16
TOP = 32000.0
S03, S01, S02, X1, D1, S11, S12, X2, D2, S21 = range(10)
GROUPS = ((0, 0), (S03, S03 + 1), (S01, S02 + 1), (X1, D1 + 1), (S11, S12 + 1), (X2, S21 + 1))
AWAY = 3
L0K1, L0K2, L1K1, L2HOME, L1HOME, L0HOME, SLOTS = 0, 1, 4, 5, 7, 11, 19


def split(x):
    hi = x.astype(BF16)
    return hi, (x - hi.astype(F32)).astype(BF16)


def dot_nt(a, b):
    return lax.dot_general(a, b, (((1,), (1,)), ((), ())), preferred_element_type=F32)


def code(x):
    peak = jnp.maximum(jnp.max(jnp.abs(x), axis=1, keepdims=True), 1e-30)
    power = jnp.ceil(jnp.log(peak) * 1.4426950408889634 + 1e-3)
    return jnp.round(x * (jnp.exp2(-power) * TOP)), power


def to_int16(x):
    return x.astype(jnp.int32).astype(jnp.int16)


def kernel(
    rhs_ref, diag_ref, panels_ref, targets_ref, counts_ref, out_ref,
    rhs, diag, panels, targets, counts, coded, away, first, sent, came, pair, mid, fin, res,
    load_sem, send_sem, near_recv, sib_recv, home_recv, k_recv, low_recv, mid_recv, fin_recv, chain,
):
    s = lax.axis_index("snode")
    q = lax.axis_index("rowblk")
    sib = q + 1 - 2 * lax.rem(q, 2)
    sx = lax.rem(s + 32, 64)
    u2, u4, u8 = lax.rem(s, 2), lax.rem(s, 4), lax.rem(s, 8)

    loads = [
        pltpu.make_async_copy(panels_ref.at[h, 0], panels.at[h], load_sem.at[h]) for h in range(3)
    ] + [
        pltpu.make_async_copy(rhs_ref.at[:, 0], rhs, load_sem.at[3]),
        pltpu.make_async_copy(diag_ref.at[:, 0], diag, load_sem.at[4]),
        pltpu.make_async_copy(targets_ref, targets, load_sem.at[5]),
        pltpu.make_async_copy(counts_ref, counts, load_sem.at[6]),
    ]
    for i in (5, 6, 3, 4, 0, 1, 2):
        loads[i].start()

    barrier = pltpu.get_barrier_semaphore()

    def tell(node, row):
        pl.semaphore_signal(barrier, inc=1, device_id=(node, row), device_id_type=MESH)

    for i in (4, 3, 5, 2, 6, 7, 1):
        tell(s, lax.rem(q + i, 8))
    tell(sx, q)

    @pl.when(u8 != 0)
    def _():
        tell(s - 1, q)

    def hand_on(step):
        @pl.when(step & (u8 != 0))
        def _():
            pl.semaphore_wait(chain, 1)

        @pl.when(step & (u8 != 7))
        def _():
            pl.semaphore_signal(chain, inc=1, device_id=(s + 1, q), device_id_type=MESH)


    def put(slot, x, buffer, at):
        whole, power = code(x)
        if at is None:
            buffer[slot] = to_int16(whole)
        else:
            buffer[at, slot] = to_int16(whole)
        return power

    def panel_sums(h):
        kinds = 3 - h
        sums = [jnp.zeros((32, 256), F32) for _ in range(kinds)]
        for b in range(32):
            block = panels[h, b].astype(F32)
            distance = lax.shift_right_logical(targets[h, 0, b], 6) - h
            alive = b < counts[h]
            for k in range(kinds):
                sums[k] = sums[k] + block * jnp.where(alive & (distance == k + 1), 1.0, 0.0)
        return sums

    def scales_of(powers, width, at):
        extra = jnp.zeros((32, width), F32)
        where = lax.broadcasted_iota(jnp.int32, (32, width), 1)
        for i, p in enumerate(powers):
            extra = jnp.where(where == at + i, p, extra)
        return extra

    def wide_heads(buffer, at, left, right, powers):
        buffer[(*at, slice(None), slice(0, 128))] = to_int16(jnp.concatenate([left, right], axis=1))
        buffer[(*at, slice(None), slice(128, 256))] = to_int16(scales_of(powers, 128, 0))

    loads[3].wait()
    loads[4].wait()
    d0_code, p_d0 = code(diag[0])
    r0_code, p_r0 = code(rhs[0])
    loads[5].wait()
    loads[6].wait()
    loads[0].wait()
    s01, s02, s03 = panel_sums(0)
    p_s03 = put(S03, s03, coded, q)
    p_s01 = put(S01, s01, coded, q)
    p_s02 = put(S02, s02, coded, q)
    scales = scales_of([p_r0, p_d0, p_s03, p_s01, p_s02], 64, 0)
    first[q, 0:32] = to_int16(d0_code)
    heads0 = to_int16(jnp.concatenate([r0_code, scales], axis=1))
    first[q, 32:48, 0:128] = heads0[0:16]
    first[q, 32:48, 128:256] = heads0[16:32]
    res[1] = jnp.zeros((8, 256), F32)
    res[2] = jnp.zeros((8, 256), F32)

    pl.semaphore_wait(barrier, jnp.where(u8 == 7, 8, 9))

    def part(g, b):
        lo, hi = GROUPS[g]
        return coded.at[b, lo:hi] if hi else first.at[b]

    def blocks(g, n):
        lo, hi = GROUPS[g]
        return coded.at[0:n, lo:hi] if hi else first.at[0:n]

    def total(view, sem):
        return pltpu.make_async_remote_copy(
            src_ref=view, dst_ref=view, send_sem=sem, recv_sem=sem,
            device_id=(s, sib), device_id_type=MESH,
        )

    def copy(g, b, row, recv):
        return pltpu.make_async_remote_copy(
            src_ref=part(g, b), dst_ref=part(g, b), send_sem=send_sem.at[1 if g == 0 else 0],
            recv_sem=recv, device_id=(s, row), device_id_type=MESH,
        )

    near = lambda g, i: near_recv.at[i - 1 if g == 0 else g + 2]

    def send_group(g):
        for i in (2, 1, 3):
            copy(g, q, lax.rem(q + 2 * i, 8), near(g, i)).start()
        copy(g, q, sib, sib_recv.at[g]).start()

    def forward(g):
        if g:
            total(blocks(g, 3), near(g, 1)).wait_recv()
        for i in (1, 3, 2):
            b = lax.rem(q + 8 - 2 * i, 8)
            if g == 0:
                copy(g, b, sib, near(g, i)).wait_recv()
            copy(g, b, sib, sib_recv.at[g]).start()

    def from_sibling(g):
        total(blocks(g, 4), sib_recv.at[g]).wait_recv()

    peer = lambda i: lax.rem(q + i, 8)

    def spread(buffer, to, send, recv, row):
        return pltpu.make_async_remote_copy(
            src_ref=buffer, dst_ref=to.at[q], send_sem=send,
            recv_sem=recv, device_id=(s, row), device_id_type=MESH,
        )

    mid_copy = lambda row: spread(pair, mid, send_sem.at[1], mid_recv, row)
    fin_copy = lambda row: spread(res.at[3], fin, send_sem.at[1], fin_recv, row)

    send_group(0)
    send_group(1)
    hand_on(u8 == 0)
    p_d1 = put(D1 - X1, diag[1], away, None)
    r1_code, p_r1 = code(rhs[1])
    loads[1].wait()
    s11, s12 = panel_sums(1)
    p_s11 = put(S11 - X1, s11, away, None)
    p_s12 = put(S12 - X1, s12, away, None)
    wide_heads(away, (0,), r1_code, jnp.zeros((32, 64), F32), [p_r1, p_d1, p_s11, p_s12])
    moves = [
        pltpu.make_async_remote_copy(
            src_ref=away.at[2 * i:2 * i + 2], dst_ref=part(AWAY + i, q), send_sem=send_sem.at[1],
            recv_sem=home_recv.at[i], device_id=(sx, q), device_id_type=MESH,
        )
        for i in range(2)
    ]
    for move in moves:
        move.start()
    send_group(2)
    p_d2 = put(D2, diag[2], coded, q)
    r2_code, p_r2 = code(rhs[2])
    r3_code, p_r3 = code(rhs[3])
    loads[2].wait()
    (s21,) = panel_sums(2)
    p_s21 = put(S21, s21, coded, q)
    wide_heads(coded, (q, X2), r2_code, r3_code, [p_r2, p_r3, p_d2, p_s21])
    hand_on((u8 > 0) & (u8 < 5))
    forward(0)
    @pl.when(lax.rem(q, 2) == 1)
    def _():
        forward(1)

    for i, move in enumerate(moves):
        move.wait_recv()
        send_group(AWAY + i)
    send_group(5)
    hand_on((u8 == 5) | (u8 == 6))

    def whole(x):
        return x.reshape(256, x.shape[2]).astype(jnp.int32).astype(F32)

    def matrix(m):
        return whole(coded[:, m])

    def apply(numbers, lhs, scale):
        hi, lo = split(numbers)
        got = dot_nt(lhs, hi) + dot_nt(lhs, lo)
        if lhs.shape[0] == 16:
            got = got[0:8] + got[8:16]
        return got * scale

    def both(x):
        hi = x.astype(BF16).astype(F32)
        return jnp.concatenate([hi, x - hi], axis=0).astype(BF16)

    def read_heads(x, at):
        row = lax.broadcasted_iota(jnp.int32, (32, x.shape[1]), 0)
        pick_lane = lax.broadcasted_iota(jnp.int32, (32, x.shape[1]), 1)
        wanted = jnp.where(row < 16, 8 * q + jnp.where(row < 8, row, row + 56), row - 16 + at)
        picker = jnp.where(pick_lane == wanted, 1.0, 0.0).astype(BF16)
        hi, lo = split(x)
        got = dot_nt(picker, hi) + dot_nt(picker, lo)
        return got[0:8], got[8:16], jnp.exp2(got[16:32]) * (1.0 / TOP)

    family = {L0K1: 0, L0K2: 1, L1K1: 2, L2HOME: 3, L1HOME: 4, L0HOME: 5}
    sharing = (1, 2, 3, 2, 1, 1)

    def k_copy(kind, first_slot, offset, node):
        return pltpu.make_async_remote_copy(
            src_ref=sent.at[kind], dst_ref=came.at[first_slot + offset], send_sem=send_sem.at[sharing[kind]],
            recv_sem=k_recv.at[family[first_slot]], device_id=(node, q), device_id_type=MESH,
        )

    def push(kind, update, level, slot, low_bits):
        @pl.when(low_bits == 0)
        def _():
            res[level] -= update

        @pl.when(low_bits != 0)
        def _():
            sent[kind] = update
            k_copy(kind, slot, jnp.maximum(low_bits - 1, 0), s - low_bits).start()

    def push_home(kind, update, slot, low_bits):
        sent[kind] = update
        k_copy(kind, slot, low_bits, lax.rem(s - low_bits + 32, 64)).start()

    def pull(level, slot, count, low_bits):
        @pl.when(low_bits == 0)
        def _():
            total(came.at[slot:slot + count], k_recv.at[family[slot]]).wait_recv()
            for i in range(count):
                res[level] -= came[slot + i]

    from_sibling(0)
    whole0 = whole(jnp.concatenate([first[:, 32:48, 0:128], first[:, 32:48, 128:256]], axis=1))
    r0, _, scales0 = read_heads(whole0, 64)
    lhs0 = both(r0 * scales0[0:1])
    x0 = apply(whole(first[:, 0:32]), lhs0, scales0[1:2]).astype(BF16)
    @pl.when(lax.rem(q, 2) == 0)
    def _():
        forward(1)

    from_sibling(1)
    hand_on(u8 == 7)
    push_home(0, apply(matrix(S03), x0, scales0[2:3]), L0HOME, u8)
    forward(2)
    start = whole0[:, 0:64] * (jnp.exp2(whole0[:, 64:65]) * (1.0 / TOP))
    dh, dl = split(diag[0])
    ch, cl = split(start)
    dot = lambda a, b: jnp.dot(a, b, preferred_element_type=F32)
    out_ref[0, 0] = dot(dh, ch) + (dot(dh, cl) + dot(dl, ch))
    from_sibling(2)
    push(1, apply(matrix(S01), x0, scales0[3:4]), 1, L0K1, u2)
    push(2, apply(matrix(S02), x0, scales0[4:5]), 2, L0K2, u4)

    forward(AWAY)
    forward(AWAY + 1)
    from_sibling(AWAY)
    r1, _, scales1 = read_heads(matrix(X1), 128)
    res[1] += r1 * scales1[0:1]
    pull(1, L0K1, 1, u2)
    x1 = apply(matrix(D1), both(res[1]), scales1[1:2]).astype(BF16)
    from_sibling(AWAY + 1)
    push(3, apply(matrix(S11), x1, scales1[2:3]), 2, L1K1, u2)
    push_home(4, apply(matrix(S12), x1, scales1[3:4]), L1HOME, u4)
    back = pltpu.make_async_remote_copy(
        src_ref=res.at[1], dst_ref=pair.at[1], send_sem=send_sem.at[1], recv_sem=low_recv,
        device_id=(sx, q), device_id_type=MESH,
    )
    back.start()
    forward(5)
    from_sibling(5)
    r2, r3, scales2 = read_heads(matrix(X2), 128)
    res[2] += r2 * scales2[0:1]
    res[3] = r3 * scales2[1:2]
    pull(2, L0K2, 3, u4)
    pull(2, L1K1, 1, u2)
    x2 = apply(matrix(D2), both(res[2]), scales2[2:3]).astype(BF16)
    push_home(5, apply(matrix(S21), x2, scales2[3:4]), L2HOME, u2)
    pair[0] = res[2]
    back.wait_recv()
    for i in range(1, 8):
        mid_copy(peer(i)).start()
    mid[q] = pair[...]

    pull(3, L1HOME, 4, u4)
    pull(3, L2HOME, 2, u2)
    pull(3, L0HOME, 8, u8)
    for i in (4, 3, 5, 2, 6, 7, 1):
        fin_copy(peer(i)).start()
    fin[q] = res[3]

    def own_rows(h, columns):
        dh, dl = split(diag[h])
        ch, cl = split(columns.reshape(64, 256))
        out_ref[h, 0] = dot_nt(dh, ch) + (dot_nt(dh, cl) + dot_nt(dl, ch))

    total(mid.at[0:7], mid_recv).wait_recv()
    own_rows(1, mid[:, 1])
    own_rows(2, mid[:, 0])
    total(fin.at[0:7], fin_recv).wait_recv()
    own_rows(3, fin[...])

    total(coded.at[0:7], send_sem.at[0]).wait_send()
    total(coded.at[0:3, 0:9], send_sem.at[1]).wait_send()

    @pl.when(u2 != 0)
    def _():
        total(sent.at[0:2], send_sem.at[2]).wait_send()

    @pl.when(u4 != 0)
    def _():
        total(sent.at[0:1], send_sem.at[3]).wait_send()


def shards(rhs, diag_inverse, panels, targets, counts):
    hbm = pl.BlockSpec(memory_space=pltpu.HBM)
    dma = pltpu.SemaphoreType.DMA
    return pl.pallas_call(
        kernel,
        out_shape=pltpu.VMEM((4, 1, 32, 64), F32),
        in_specs=[hbm] * 5,
        out_specs=pl.BlockSpec(memory_space=pltpu.VMEM),
        scratch_shapes=[
            pltpu.VMEM((4, 32, 64), F32),
            pltpu.VMEM((4, 32, 256), F32),
            pltpu.VMEM((3, 32, 32, 256), BF16),
            pltpu.SMEM((3, 1, 32), jnp.int32),
            pltpu.SMEM((3,), jnp.int32),
            pltpu.VMEM((8, 10, 32, 256), jnp.int16),
            pltpu.VMEM((4, 32, 256), jnp.int16),
            pltpu.VMEM((8, 48, 256), jnp.int16),
            pltpu.VMEM((6, 8, 256), F32),
            pltpu.VMEM((SLOTS, 8, 256), F32),
            pltpu.VMEM((2, 8, 256), F32),
            pltpu.VMEM((8, 2, 8, 256), F32),
            pltpu.VMEM((8, 8, 256), F32),
            pltpu.VMEM((4, 8, 256), F32),
            dma((7,)),
            dma((4,)),
            dma((8,)),
            dma((6,)),
            dma((2,)),
            dma((6,)),
            dma(()),
            dma(()),
            dma(()),
            pltpu.SemaphoreType.REGULAR,
        ],
        compiler_params=pltpu.CompilerParams(
            collective_id=0, has_side_effects=True, vmem_limit_bytes=62 * 1024 * 1024
        ),
        name="substitute",
    )(rhs, diag_inverse, panels, targets, counts[:, 0])


def solution(mesh):
    in_specs = (
        P(None, "snode", "rowblk", None),
        P(None, "snode", "rowblk", None),
        P(None, "snode", None, "rowblk", None),
        P(None, "snode", None),
        P(None, "snode"),
    )
    out_specs = P(None, "snode", "rowblk", None)
    return jax.shard_map(shards, mesh=mesh, in_specs=in_specs, out_specs=out_specs, check_vma=False)
```

```python
import jax
import jax.numpy as jnp
from jax import lax
from jax.experimental import pallas as pl
from jax.experimental.pallas import tpu as pltpu
from jax.sharding import PartitionSpec as P

MESH = pl.DeviceIdType.MESH
F32, BF16 = jnp.float32, jnp.bfloat16
TOP = 32000.0
S03, S01, S02, X1, D1, S11, S12, X2, D2, S21 = range(10)
GROUPS = ((0, 0), (S03, S03 + 1), (S01, S02 + 1), (X1, D1 + 1), (S11, S12 + 1), (X2, S21 + 1))
AWAY = 3
L0K1, L0K2, L1K1, L2HOME, L1HOME, L0HOME, SLOTS = 0, 1, 4, 5, 7, 11, 19


def split(x):
    hi = x.astype(BF16)
    return hi, (x - hi.astype(F32)).astype(BF16)


def dot_nt(a, b):
    return lax.dot_general(a, b, (((1,), (1,)), ((), ())), preferred_element_type=F32)


def code(x):
    peak = jnp.maximum(jnp.max(jnp.abs(x), axis=1, keepdims=True), 1e-30)
    power = jnp.ceil(jnp.log(peak) * 1.4426950408889634 + 1e-3)
    return jnp.round(x * (jnp.exp2(-power) * TOP)), power


def to_int16(x):
    return x.astype(jnp.int32).astype(jnp.int16)


def kernel(
    rhs_ref, diag_ref, panels_ref, targets_ref, counts_ref, out_ref,
    rhs, diag, panels, targets, counts, coded, away, first, sent, came, pair, mid, fin, res,
    load_sem, send_sem, near_recv, sib_recv, home_recv, k_recv, low_recv, mid_recv, fin_recv, chain,
):
    s = lax.axis_index("snode")
    q = lax.axis_index("rowblk")
    sib = q + 1 - 2 * lax.rem(q, 2)
    sx = lax.rem(s + 32, 64)
    u2, u4, u8 = lax.rem(s, 2), lax.rem(s, 4), lax.rem(s, 8)

    loads = [
        pltpu.make_async_copy(panels_ref.at[h, 0], panels.at[h], load_sem.at[h]) for h in range(3)
    ] + [
        pltpu.make_async_copy(rhs_ref.at[:, 0], rhs, load_sem.at[3]),
        pltpu.make_async_copy(diag_ref.at[:, 0], diag, load_sem.at[4]),
        pltpu.make_async_copy(targets_ref, targets, load_sem.at[5]),
        pltpu.make_async_copy(counts_ref, counts, load_sem.at[6]),
    ]
    for i in (5, 6, 3, 4, 0, 1, 2):
        loads[i].start()

    barrier = pltpu.get_barrier_semaphore()

    def tell(node, row):
        pl.semaphore_signal(barrier, inc=1, device_id=(node, row), device_id_type=MESH)

    for i in (4, 3, 5, 2, 6, 7, 1):
        tell(s, lax.rem(q + i, 8))
    tell(sx, q)

    @pl.when(u8 != 0)
    def _():
        tell(s - 1, q)

    def hand_on(step):
        @pl.when(step & (u8 != 0))
        def _():
            pl.semaphore_wait(chain, 1)

        @pl.when(step & (u8 != 7))
        def _():
            pl.semaphore_signal(chain, inc=1, device_id=(s + 1, q), device_id_type=MESH)


    def put(slot, x, buffer, at):
        whole, power = code(x)
        if at is None:
            buffer[slot] = to_int16(whole)
        else:
            buffer[at, slot] = to_int16(whole)
        return power

    def panel_sums(h):
        kinds = 3 - h
        sums = [jnp.zeros((32, 256), F32) for _ in range(kinds)]
        for b in range(32):
            block = panels[h, b].astype(F32)
            distance = lax.shift_right_logical(targets[h, 0, b], 6) - h
            alive = b < counts[h]
            for k in range(kinds):
                sums[k] = sums[k] + block * jnp.where(alive & (distance == k + 1), 1.0, 0.0)
        return sums

    def scales_of(powers, width, at):
        extra = jnp.zeros((32, width), F32)
        where = lax.broadcasted_iota(jnp.int32, (32, width), 1)
        for i, p in enumerate(powers):
            extra = jnp.where(where == at + i, p, extra)
        return extra

    def wide_heads(buffer, at, left, right, powers):
        buffer[(*at, slice(None), slice(0, 128))] = to_int16(jnp.concatenate([left, right], axis=1))
        buffer[(*at, slice(None), slice(128, 256))] = to_int16(scales_of(powers, 128, 0))

    loads[3].wait()
    loads[4].wait()
    d0_code, p_d0 = code(diag[0])
    r0_code, p_r0 = code(rhs[0])
    loads[5].wait()
    loads[6].wait()
    loads[0].wait()
    s01, s02, s03 = panel_sums(0)
    p_s03 = put(S03, s03, coded, q)
    p_s01 = put(S01, s01, coded, q)
    p_s02 = put(S02, s02, coded, q)
    scales = scales_of([p_r0, p_d0, p_s03, p_s01, p_s02], 64, 0)
    first[q, 0:32] = to_int16(d0_code)
    heads0 = to_int16(jnp.concatenate([r0_code, scales], axis=1))
    first[q, 32:48, 0:128] = heads0[0:16]
    first[q, 32:48, 128:256] = heads0[16:32]
    res[1] = jnp.zeros((8, 256), F32)
    res[2] = jnp.zeros((8, 256), F32)

    pl.semaphore_wait(barrier, jnp.where(u8 == 7, 8, 9))

    def part(g, b):
        lo, hi = GROUPS[g]
        return coded.at[b, lo:hi] if hi else first.at[b]

    def blocks(g, n):
        lo, hi = GROUPS[g]
        return coded.at[0:n, lo:hi] if hi else first.at[0:n]

    def total(view, sem):
        return pltpu.make_async_remote_copy(
            src_ref=view, dst_ref=view, send_sem=sem, recv_sem=sem,
            device_id=(s, sib), device_id_type=MESH,
        )

    def copy(g, b, row, recv):
        return pltpu.make_async_remote_copy(
            src_ref=part(g, b), dst_ref=part(g, b), send_sem=send_sem.at[1 if g == 0 else 0],
            recv_sem=recv, device_id=(s, row), device_id_type=MESH,
        )

    near = lambda g, i: near_recv.at[i - 1 if g == 0 else g + 2]

    def send_group(g):
        for i in (2, 1, 3):
            copy(g, q, lax.rem(q + 2 * i, 8), near(g, i)).start()
        copy(g, q, sib, sib_recv.at[g]).start()

    def forward(g):
        if g:
            total(blocks(g, 3), near(g, 1)).wait_recv()
        for i in (1, 3, 2):
            b = lax.rem(q + 8 - 2 * i, 8)
            if g == 0:
                copy(g, b, sib, near(g, i)).wait_recv()
            copy(g, b, sib, sib_recv.at[g]).start()

    def from_sibling(g):
        total(blocks(g, 4), sib_recv.at[g]).wait_recv()

    peer = lambda i: lax.rem(q + i, 8)

    def spread(buffer, to, send, recv, row):
        return pltpu.make_async_remote_copy(
            src_ref=buffer, dst_ref=to.at[q], send_sem=send,
            recv_sem=recv, device_id=(s, row), device_id_type=MESH,
        )

    mid_copy = lambda row: spread(pair, mid, send_sem.at[1], mid_recv, row)
    fin_copy = lambda row: spread(res.at[3], fin, send_sem.at[1], fin_recv, row)

    send_group(0)
    send_group(1)
    hand_on(u8 == 0)
    p_d1 = put(D1 - X1, diag[1], away, None)
    r1_code, p_r1 = code(rhs[1])
    loads[1].wait()
    s11, s12 = panel_sums(1)
    p_s11 = put(S11 - X1, s11, away, None)
    p_s12 = put(S12 - X1, s12, away, None)
    wide_heads(away, (0,), r1_code, jnp.zeros((32, 64), F32), [p_r1, p_d1, p_s11, p_s12])
    moves = [
        pltpu.make_async_remote_copy(
            src_ref=away.at[2 * i:2 * i + 2], dst_ref=part(AWAY + i, q), send_sem=send_sem.at[1],
            recv_sem=home_recv.at[i], device_id=(sx, q), device_id_type=MESH,
        )
        for i in range(2)
    ]
    for move in moves:
        move.start()
    send_group(2)
    p_d2 = put(D2, diag[2], coded, q)
    r2_code, p_r2 = code(rhs[2])
    r3_code, p_r3 = code(rhs[3])
    loads[2].wait()
    (s21,) = panel_sums(2)
    p_s21 = put(S21, s21, coded, q)
    wide_heads(coded, (q, X2), r2_code, r3_code, [p_r2, p_r3, p_d2, p_s21])
    hand_on((u8 > 0) & (u8 < 5))
    forward(0)
    @pl.when(lax.rem(q, 2) == 1)
    def _():
        forward(1)

    for i, move in enumerate(moves):
        move.wait_recv()
        send_group(AWAY + i)
    send_group(5)
    hand_on((u8 == 5) | (u8 == 6))

    def whole(x):
        return x.reshape(256, x.shape[2]).astype(jnp.int32).astype(F32)

    def matrix(m):
        return whole(coded[:, m])

    def apply(numbers, lhs, scale):
        hi, lo = split(numbers)
        got = dot_nt(lhs, hi) + dot_nt(lhs, lo)
        if lhs.shape[0] == 16:
            got = got[0:8] + got[8:16]
        return got * scale

    def both(x):
        hi = x.astype(BF16).astype(F32)
        return jnp.concatenate([hi, x - hi], axis=0).astype(BF16)

    def read_heads(x, at):
        row = lax.broadcasted_iota(jnp.int32, (32, x.shape[1]), 0)
        pick_lane = lax.broadcasted_iota(jnp.int32, (32, x.shape[1]), 1)
        wanted = jnp.where(row < 16, 8 * q + jnp.where(row < 8, row, row + 56), row - 16 + at)
        picker = jnp.where(pick_lane == wanted, 1.0, 0.0).astype(BF16)
        hi, lo = split(x)
        got = dot_nt(picker, hi) + dot_nt(picker, lo)
        return got[0:8], got[8:16], jnp.exp2(got[16:32]) * (1.0 / TOP)

    family = {L0K1: 0, L0K2: 1, L1K1: 2, L2HOME: 3, L1HOME: 4, L0HOME: 5}
    sharing = (1, 2, 3, 2, 1, 1)

    def k_copy(kind, first_slot, offset, node):
        return pltpu.make_async_remote_copy(
            src_ref=sent.at[kind], dst_ref=came.at[first_slot + offset], send_sem=send_sem.at[sharing[kind]],
            recv_sem=k_recv.at[family[first_slot]], device_id=(node, q), device_id_type=MESH,
        )

    def push(kind, update, level, slot, low_bits):
        @pl.when(low_bits == 0)
        def _():
            res[level] -= update

        @pl.when(low_bits != 0)
        def _():
            sent[kind] = update
            k_copy(kind, slot, jnp.maximum(low_bits - 1, 0), s - low_bits).start()

    def push_home(kind, update, slot, low_bits):
        sent[kind] = update
        k_copy(kind, slot, low_bits, lax.rem(s - low_bits + 32, 64)).start()

    def pull(level, slot, count, low_bits):
        @pl.when(low_bits == 0)
        def _():
            total(came.at[slot:slot + count], k_recv.at[family[slot]]).wait_recv()
            for i in range(count):
                res[level] -= came[slot + i]

    from_sibling(0)
    whole0 = whole(jnp.concatenate([first[:, 32:48, 0:128], first[:, 32:48, 128:256]], axis=1))
    r0, _, scales0 = read_heads(whole0, 64)
    lhs0 = both(r0 * scales0[0:1])
    x0 = apply(whole(first[:, 0:32]), lhs0, scales0[1:2]).astype(BF16)
    @pl.when(lax.rem(q, 2) == 0)
    def _():
        forward(1)

    from_sibling(1)
    hand_on(u8 == 7)
    push_home(0, apply(matrix(S03), x0, scales0[2:3]), L0HOME, u8)
    forward(2)
    start = whole0[:, 0:64] * (jnp.exp2(whole0[:, 64:65]) * (1.0 / TOP))
    dh, dl = split(diag[0])
    ch, cl = split(start)
    dot = lambda a, b: jnp.dot(a, b, preferred_element_type=F32)
    out_ref[0, 0] = dot(dh, ch) + (dot(dh, cl) + dot(dl, ch))
    from_sibling(2)
    push(1, apply(matrix(S01), x0, scales0[3:4]), 1, L0K1, u2)
    push(2, apply(matrix(S02), x0, scales0[4:5]), 2, L0K2, u4)

    forward(AWAY)
    forward(AWAY + 1)
    from_sibling(AWAY)
    r1, _, scales1 = read_heads(matrix(X1), 128)
    res[1] += r1 * scales1[0:1]
    pull(1, L0K1, 1, u2)
    x1 = apply(matrix(D1), both(res[1]), scales1[1:2]).astype(BF16)
    from_sibling(AWAY + 1)
    push(3, apply(matrix(S11), x1, scales1[2:3]), 2, L1K1, u2)
    push_home(4, apply(matrix(S12), x1, scales1[3:4]), L1HOME, u4)
    back = pltpu.make_async_remote_copy(
        src_ref=res.at[1], dst_ref=pair.at[1], send_sem=send_sem.at[1], recv_sem=low_recv,
        device_id=(sx, q), device_id_type=MESH,
    )
    back.start()
    forward(5)
    from_sibling(5)
    r2, r3, scales2 = read_heads(matrix(X2), 128)
    res[2] += r2 * scales2[0:1]
    res[3] = r3 * scales2[1:2]
    pull(2, L0K2, 3, u4)
    pull(2, L1K1, 1, u2)
    x2 = apply(matrix(D2), both(res[2]), scales2[2:3]).astype(BF16)
    push_home(5, apply(matrix(S21), x2, scales2[3:4]), L2HOME, u2)
    pair[0] = res[2]
    back.wait_recv()
    for i in range(1, 8):
        mid_copy(peer(i)).start()
    mid[q] = pair[...]

    pull(3, L1HOME, 4, u4)
    pull(3, L2HOME, 2, u2)
    pull(3, L0HOME, 8, u8)
    for even, odd in ((5, 3), (4, 4), (3, 1), (7, 5), (2, 2), (6, 6), (1, 7)):
        fin_copy(peer(jnp.where(lax.rem(q, 2) == 0, even, odd))).start()
    fin[q] = res[3]

    def own_rows(h, columns):
        dh, dl = split(diag[h])
        ch, cl = split(columns.reshape(64, 256))
        out_ref[h, 0] = dot_nt(dh, ch) + (dot_nt(dh, cl) + dot_nt(dl, ch))

    total(mid.at[0:7], mid_recv).wait_recv()
    own_rows(1, mid[:, 1])
    own_rows(2, mid[:, 0])
    total(fin.at[0:7], fin_recv).wait_recv()
    own_rows(3, fin[...])

    total(coded.at[0:7], send_sem.at[0]).wait_send()
    total(coded.at[0:3, 0:9], send_sem.at[1]).wait_send()

    @pl.when(u2 != 0)
    def _():
        total(sent.at[0:2], send_sem.at[2]).wait_send()

    @pl.when(u4 != 0)
    def _():
        total(sent.at[0:1], send_sem.at[3]).wait_send()


def shards(rhs, diag_inverse, panels, targets, counts):
    hbm = pl.BlockSpec(memory_space=pltpu.HBM)
    dma = pltpu.SemaphoreType.DMA
    return pl.pallas_call(
        kernel,
        out_shape=pltpu.VMEM((4, 1, 32, 64), F32),
        in_specs=[hbm] * 5,
        out_specs=pl.BlockSpec(memory_space=pltpu.VMEM),
        scratch_shapes=[
            pltpu.VMEM((4, 32, 64), F32),
            pltpu.VMEM((4, 32, 256), F32),
            pltpu.VMEM((3, 32, 32, 256), BF16),
            pltpu.SMEM((3, 1, 32), jnp.int32),
            pltpu.SMEM((3,), jnp.int32),
            pltpu.VMEM((8, 10, 32, 256), jnp.int16),
            pltpu.VMEM((4, 32, 256), jnp.int16),
            pltpu.VMEM((8, 48, 256), jnp.int16),
            pltpu.VMEM((6, 8, 256), F32),
            pltpu.VMEM((SLOTS, 8, 256), F32),
            pltpu.VMEM((2, 8, 256), F32),
            pltpu.VMEM((8, 2, 8, 256), F32),
            pltpu.VMEM((8, 8, 256), F32),
            pltpu.VMEM((4, 8, 256), F32),
            dma((7,)),
            dma((4,)),
            dma((8,)),
            dma((6,)),
            dma((2,)),
            dma((6,)),
            dma(()),
            dma(()),
            dma(()),
            pltpu.SemaphoreType.REGULAR,
        ],
        compiler_params=pltpu.CompilerParams(
            collective_id=0, has_side_effects=True, vmem_limit_bytes=62 * 1024 * 1024
        ),
        name="substitute",
    )(rhs, diag_inverse, panels, targets, counts[:, 0])


def solution(mesh):
    in_specs = (
        P(None, "snode", "rowblk", None),
        P(None, "snode", "rowblk", None),
        P(None, "snode", None, "rowblk", None),
        P(None, "snode", None),
        P(None, "snode"),
    )
    out_specs = P(None, "snode", "rowblk", None)
    return jax.shard_map(shards, mesh=mesh, in_specs=in_specs, out_specs=out_specs, check_vma=False)
```
